32 devices in a mesh: rows: 4 (over x, core), images: 8 (over z, y).
Axes of the slice: x: 2, y: 2, z: 4, core: 2. Of those that a mesh axis runs over, the one named last changes fastest.
Arguments:
- features: bfloat16 [4, 32, 16, 16, 1024], P(None, 'images', 'rows'), may hold values from -6 to 6
- crop_rows: int32 [4, 32], P(None, 'images'), may hold values from 8 to 16, as said below
- crop_cols: int32 [4, 32], P(None, 'images'), may hold values from 8 to 16
- one_reduce: bfloat16 [1024, 256], replicated, may hold values from -0.1875 to 0.1875
- one_reduce_norm: float32 [256, 2], replicated, may hold values from 0.5 to 1.5
- one_spatial: bfloat16 [256, 9, 256], replicated, may hold values from -0.125 to 0.125
- one_spatial_norm: float32 [256, 2], replicated, may hold values from 0.5 to 1.5
- one_expand: bfloat16 [256, 1024], replicated, may hold values from -0.375 to 0.375
- one_expand_norm: float32 [1024, 2], replicated, may hold values from 0.5 to 1.5
- two_reduce: bfloat16 [1024, 512], replicated, may hold values from -0.1875 to 0.1875
- two_reduce_norm: float32 [512, 2], replicated, may hold values from 0.5 to 1.5
- two_spatial: bfloat16 [512, 9, 512], replicated, may hold values from -0.09375 to 0.09375
- two_spatial_norm: float32 [512, 2], replicated, may hold values from 0.5 to 1.5
- two_expand: bfloat16 [512, 2048], replicated, may hold values from -0.25 to 0.25
- two_expand_norm: float32 [2048, 2], replicated, may hold values from 0.5 to 1.5
- two_shortcut: bfloat16 [1024, 2048], replicated, may hold values from -0.1875 to 0.1875
- two_shortcut_norm: float32 [2048, 2], replicated, may hold values from 0.5 to 1.5
- out_grad: bfloat16 [4, 32, 8, 8, 2048], P(None, 'images', 'rows'), may hold values from -6 to 6
Outputs:
- block_out: bfloat16 [4, 32, 8, 8, 2048], P(None, 'images', 'rows')
- features_grad: bfloat16 [4, 32, 16, 16, 1024], P(None, 'images', 'rows')
- one_reduce_grad: float32 [1024, 256], P('images')
- one_reduce_norm_grad: float32 [256, 2], P('images')
- one_spatial_grad: float32 [256, 9, 256], P('images')
- one_spatial_norm_grad: float32 [256, 2], P('images')
- one_expand_grad: float32 [256, 1024], P('images')
- one_expand_norm_grad: float32 [1024, 2], P('images')
- two_reduce_grad: float32 [1024, 512], P('images')
- two_reduce_norm_grad: float32 [512, 2], P('images')
- two_spatial_grad: float32 [512, 9, 512], P('images')
- two_spatial_norm_grad: float32 [512, 2], P('images')
- two_expand_grad: float32 [512, 2048], P('images')
- two_expand_norm_grad: float32 [2048, 2], P('images')
- two_shortcut_grad: float32 [1024, 2048], P('images')
- two_shortcut_norm_grad: float32 [2048, 2], P('images')
The draws below stay inside these ranges and needn't reach their ends.
Inputs may be any that keep to these rules, and one draw needn't show every extreme that they name: `crop_rows`: within each micro-batch, each aligned run of 4 crops holds one crop with all 16 rows valid.
All inputs are finite; a program needn't handle non-finite values.
Results may differ from the reference program's by a relative error of at most 0.017.
Values may be sent and summed in bfloat16 or wider, within the bound.
No kernel may reach another device: no remote copies, remote signals or barrier semaphores. Data moves between devices by JAX's collectives and lax.ppermute only.
A program may use at most 256 MiB of HBM per device.

```python
import jax
import jax.numpy as jnp
from jax import lax

CHANNELS = 1024
INNER_ONE = 256
INNER_TWO = 512
WIDE_OUT = 2048
MAP_ROWS = 16
MAP_COLS = 16
CROPS = 4
MICRO = 4
BATCH = 32
N_IMAGES = 8


def draw_crop_rows(key, part):
    key = jax.random.fold_in(key, 11)
    height_key, pick_key = jax.random.split(key)
    heights = jax.random.randint(height_key, (MICRO, BATCH // CROPS, CROPS), MAP_ROWS // 2, MAP_ROWS + 1)
    picked = jax.random.randint(pick_key, (MICRO, BATCH // CROPS, 1), 0, CROPS)
    tallest = jnp.arange(CROPS, dtype=jnp.int32)[None, None, :] == picked
    return jnp.where(tallest, MAP_ROWS, heights).reshape(MICRO, BATCH).astype(jnp.int32)


def set_ends(entries, own_key, least, largest):
    index_at = [jax.random.randint(jax.random.fold_in(own_key, axis), (), 0, length) for axis, length in enumerate(entries.shape)]
    longest = entries.shape.index(max(entries.shape))
    beside = index_at[:longest] + [(index_at[longest] + 1) % entries.shape[longest]] + index_at[longest + 1:]
    return entries.at[tuple(index_at)].set(least).at[tuple(beside)].set(largest)


def level_of(own_key, dims, shards, least, largest):
    gain, own = 1.0, jax.random.fold_in(own_key, 6)
    for position, blocks in shards:
        steps = jnp.exp(jax.random.uniform(jax.random.fold_in(own, position), (blocks,), jnp.float32, least / len(shards), largest / len(shards)))
        gain = gain * jnp.repeat(steps, dims[position] // blocks).reshape([-1 if axis == position else 1 for axis in range(len(dims))])
    return gain


def noise(stream_key, shape, deviation, reach, cuts=(), held_as=jnp.bfloat16):
    array = jax.random.normal(stream_key, shape, jnp.float32) * deviation
    if len(cuts) > 0:
        array = level_of(stream_key, shape, cuts, -0.22, 0.18) * array
    return jnp.clip(array, min=-reach, max=reach).astype(held_as)


def setup_inputs(seed: int = 0) -> dict:
    seeds = jax.random.split(jax.random.key(seed), 19)
    return {
        "features": noise(seeds[0], (MICRO, BATCH, MAP_ROWS, MAP_COLS, CHANNELS), 1.0, 6.0, ((1, 8), (2, 4))),
        "crop_rows": draw_crop_rows(jax.random.fold_in(seeds[18], 71), 0),
        "crop_cols": set_ends(jax.random.randint(seeds[2], (MICRO, BATCH), MAP_COLS // 2, MAP_COLS + 1), jax.random.fold_in(seeds[2], 1), MAP_COLS // 2, MAP_COLS).astype(jnp.int32),
        "one_reduce": noise(seeds[3], (CHANNELS, INNER_ONE), CHANNELS ** -0.5, 0.1875),
        "one_reduce_norm": jnp.clip(jax.random.uniform(seeds[4], (INNER_ONE, 2), jnp.float32, 0.5, 1.5), 0.5, 1.5),
        "one_spatial": noise(seeds[5], (INNER_ONE, 9, INNER_ONE), (9 * INNER_ONE) ** -0.5, 0.125),
        "one_spatial_norm": jnp.clip(jax.random.uniform(seeds[6], (INNER_ONE, 2), jnp.float32, 0.5, 1.5), 0.5, 1.5),
        "one_expand": noise(seeds[7], (INNER_ONE, CHANNELS), INNER_ONE ** -0.5, 0.375),
        "one_expand_norm": jnp.clip(jax.random.uniform(seeds[8], (CHANNELS, 2), jnp.float32, 0.5, 1.5), 0.5, 1.5),
        "two_reduce": noise(seeds[9], (CHANNELS, INNER_TWO), CHANNELS ** -0.5, 0.1875),
        "two_reduce_norm": jnp.clip(jax.random.uniform(seeds[10], (INNER_TWO, 2), jnp.float32, 0.5, 1.5), 0.5, 1.5),
        "two_spatial": noise(seeds[11], (INNER_TWO, 9, INNER_TWO), (9 * INNER_TWO) ** -0.5, 0.09375),
        "two_spatial_norm": jnp.clip(jax.random.uniform(seeds[12], (INNER_TWO, 2), jnp.float32, 0.5, 1.5), 0.5, 1.5),
        "two_expand": noise(seeds[13], (INNER_TWO, WIDE_OUT), INNER_TWO ** -0.5, 0.25),
        "two_expand_norm": jnp.clip(jax.random.uniform(seeds[14], (WIDE_OUT, 2), jnp.float32, 0.5, 1.5), 0.5, 1.5),
        "two_shortcut": noise(seeds[15], (CHANNELS, WIDE_OUT), CHANNELS ** -0.5, 0.1875),
        "two_shortcut_norm": jnp.clip(jax.random.uniform(seeds[16], (WIDE_OUT, 2), jnp.float32, 0.5, 1.5), 0.5, 1.5),
        "out_grad": noise(seeds[17], (MICRO, BATCH, MAP_ROWS // 2, MAP_COLS // 2, WIDE_OUT), 1.0, 6.0, ((1, 8), (2, 4))),
    }


@jax.custom_vjp
def low(v):
    return lax.optimization_barrier(v.astype(jnp.bfloat16)).astype(jnp.float32)

@jax.custom_vjp
def low_back(v):
    return v

def low_keep(v):
    return (low(v), None)

def low_pass(kept, grad):
    return (grad,)

def back_keep(v):
    return (v, None)

def back_low(kept, grad):
    return (low(grad),)
low.defvjp(low_keep, low_pass)
low_back.defvjp(back_keep, back_low)
epsilon = 1e-05

def pointwise(inputs, weight):
    return jnp.einsum('bhwc,cd->bhwd', inputs, weight, precision=lax.Precision.HIGHEST)

def spatial(inputs, weight, stride):
    kernel = weight.reshape(weight.shape[0], 3, 3, weight.shape[2]).transpose(1, 2, 0, 3)
    return lax.conv_general_dilated(inputs, kernel, (stride, stride), ((1, 1), (1, 1)), dimension_numbers=('NHWC', 'HWIO', 'NHWC'), precision=lax.Precision.HIGHEST)

def batch_norm(values, pixel_mask, params):
    pixels = jnp.sum(pixel_mask)
    center = lax.optimization_barrier(jnp.sum(values * pixel_mask, axis=(0, 1, 2))) / pixels
    square = lax.optimization_barrier(jnp.sum(values * values * pixel_mask, axis=(0, 1, 2))) / pixels
    return (values - center) * lax.rsqrt(square - center * center + epsilon) * params[:, 0] + params[:, 1]

def group_forward(images, rows_valid, cols_valid, one_reduce, one_reduce_norm, one_spatial, one_spatial_norm, one_expand, one_expand_norm, two_reduce, two_reduce_norm, two_spatial, two_spatial_norm, two_expand, two_expand_norm, two_shortcut, two_shortcut_norm):
    row_place = jnp.arange(MAP_ROWS, dtype=jnp.int32)
    col_place = jnp.arange(MAP_COLS, dtype=jnp.int32)
    inside = (row_place[None, :, None] < rows_valid[:, None, None]) & (col_place[None, None, :] < cols_valid[:, None, None])
    full_mask = inside.astype(jnp.float32)[..., None]
    half_mask = full_mask[:, ::2, ::2]
    inputs = images * full_mask
    active_one = low(full_mask * jax.nn.silu(batch_norm(low_back(pointwise(inputs, one_reduce)), full_mask, one_reduce_norm)))
    active_two = low(full_mask * jax.nn.silu(batch_norm(low_back(spatial(active_one, one_spatial, 1)), full_mask, one_spatial_norm)))
    branch_one = batch_norm(low_back(pointwise(active_two, one_expand)), full_mask, one_expand_norm)
    middle = low_back(low(full_mask * jax.nn.silu(inputs + branch_one)))
    active_four = low(full_mask * jax.nn.silu(batch_norm(low_back(pointwise(middle, two_reduce)), full_mask, two_reduce_norm)))
    active_five = low(half_mask * jax.nn.silu(batch_norm(low_back(spatial(active_four, two_spatial, 2)), half_mask, two_spatial_norm)))
    branch_two = batch_norm(low_back(pointwise(active_five, two_expand)), half_mask, two_expand_norm)
    shortcut = batch_norm(low_back(pointwise(middle[:, ::2, ::2], two_shortcut)), half_mask, two_shortcut_norm)
    return half_mask * jax.nn.silu(branch_two + shortcut)

def reference(features, crop_rows, crop_cols, one_reduce, one_reduce_norm, one_spatial, one_spatial_norm, one_expand, one_expand_norm, two_reduce, two_reduce_norm, two_spatial, two_spatial_norm, two_expand, two_expand_norm, two_shortcut, two_shortcut_norm, out_grad):
    groups = MICRO * N_IMAGES
    images = features.reshape(groups, CROPS, MAP_ROWS, MAP_COLS, CHANNELS)
    rows_valid = crop_rows.reshape(groups, CROPS)
    cols_valid = crop_cols.reshape(groups, CROPS)
    cotangent = out_grad.reshape(groups, CROPS, MAP_ROWS // 2, MAP_COLS // 2, WIDE_OUT)
    params = tuple((weight.astype(jnp.float32) for weight in (one_reduce, one_reduce_norm, one_spatial, one_spatial_norm, one_expand, one_expand_norm, two_reduce, two_reduce_norm, two_spatial, two_spatial_norm, two_expand, two_expand_norm, two_shortcut, two_shortcut_norm)))

    def one_group(totals, item):
        group_images, group_rows, group_cols, group_grad = item

        def forward(inputs, *weights):
            return group_forward(inputs, group_rows, group_cols, *weights)
        output, pullback = jax.vjp(forward, group_images.astype(jnp.float32), *params)
        grads = pullback(group_grad.astype(jnp.float32))
        totals = tuple((total + part for total, part in zip(totals, grads[1:])))
        return (totals, (output.astype(jnp.bfloat16), grads[0].astype(jnp.bfloat16)))
    start = tuple((jnp.zeros_like(weight) for weight in params))
    totals, (outputs, input_grads) = lax.scan(one_group, start, (images, rows_valid, cols_valid, cotangent))
    block_out = outputs.reshape(MICRO, BATCH, MAP_ROWS // 2, MAP_COLS // 2, WIDE_OUT)
    features_grad = input_grads.reshape(MICRO, BATCH, MAP_ROWS, MAP_COLS, CHANNELS)
    return (block_out, features_grad, totals[0], totals[1], totals[2], totals[3], totals[4], totals[5], totals[6], totals[7], totals[8], totals[9], totals[10], totals[11], totals[12], totals[13])
```

```python
import functools
import math

import jax
import jax.numpy as jnp
from jax import lax
from jax.experimental import pallas as pl
from jax.experimental.pallas import tpu as pltpu
from jax.sharding import PartitionSpec as P

EPSILON = 1e-05
LANES = 128
BF16, F32 = jnp.bfloat16, jnp.float32


def words(*parts):
    return " ".join(parts)


def log2(size):
    assert size & (size - 1) == 0
    return size.bit_length() - 1


def dot(left, right):
    return jnp.dot(left, right, preferred_element_type=F32)


def dot_nt(left, right):
    return lax.dot_general(left, right, (((1,), (1,)), ((), ())), preferred_element_type=F32)


def dot_tn(left, right):
    return lax.dot_general(left, right, (((0,), (0,)), ((), ())), preferred_element_type=F32)


def sigmoid(values):
    return 0.5 * jnp.tanh(0.5 * values) + 0.5


def silu(values):
    return values * sigmoid(values)


def silu_slope(values):
    gate = sigmoid(values)
    return gate * (1.0 + values * (1.0 - gate))


def wide(mask, columns):
    return jnp.concatenate([mask] * (columns // LANES), axis=1)


def fold(values):
    rows, columns = values.shape
    return jnp.sum(values.reshape(rows // 8, 8, columns), axis=0)


def total(values):
    return jnp.sum(values, axis=0, keepdims=True)


class Slot:
    def __init__(self, source, target, semaphores, here, order=(0,)):
        size = here.shape[0] // len(order)
        self.copies, self.here, self.started = {}, here, False
        for part in order:
            rows = slice(part * size, (part + 1) * size)
            self.copies[part] = pltpu.make_async_copy(source.at[rows], target.at[rows], semaphores.at[part])

    def start(self):
        if not self.started:
            for copy in self.copies.values():
                copy.start()
        self.started = True

    def wait(self, part=None):
        self.start()
        for part in list(self.copies) if part is None else [part]:
            if part in self.copies:
                self.copies.pop(part).wait()


class Arrays:
    def __init__(self, arrays):
        self.arrays = arrays
        self.slots = {name: value for name, value in arrays.items() if isinstance(value, Slot)}

    def start(self, names=None):
        for name in self.slots if names is None else names.split():
            if name in self.slots:
                self.slots[name].start()

    def wait(self):
        for slot in self.slots.values():
            slot.wait()

    def __getitem__(self, name):
        return self.slots[name].here if name in self.slots else self.arrays[name]


class Inputs(Arrays):
    def part(self, name, part):
        slot = self.slots[name]
        size = slot.here.shape[0] // len(PARTS[name])
        slot.wait(part)
        return slot.here.at[part * size : (part + 1) * size]

    def __getitem__(self, name):
        if name in self.slots:
            self.slots[name].wait()
        return super().__getitem__(name)


READS = dict(
    place="",
    first="full_mask hot phase_mask half_mask",
    second=words("mid a5 v6 v7", "half_mask"),
    five=words("dz6 a5 half_mask stats", "z5 a4 sh4 dz7", "v7"),
    four=words("hot dz5 stats z4", "phase_mask"),
    middle=words("dz4 v4 strided stats", "hot z3 xm full_mask", "mid a2"),
    last=words("dz3 v3 z2 v2", "stats full_mask hot z1", "v1 joined a1 xm", "both34 norm67 norm5 norm4", "norm3"),
)
STAGES = list(READS)


def flow(stage, body, dims, kept, inputs, outs, scratch=(), first="", far="", share=""):
    far = far.split()
    later = " ".join(READS[name] for name in STAGES[STAGES.index(stage) + 1 :]).split()
    loaded = ["v" + name[1:] for name in share.split()]
    held = [name for name in kept if name in later and name not in loaded]
    read = {name: kept[name] for name in READS[stage].split()}
    inputs = {**inputs, **read, **{name: kept[name] for name in held}}
    far_in = [name for name in inputs if name[0] == "w"]
    made = dict(outs)
    shared = {name: "v" + name[1:] for name in share.split()}
    own = [name for name in far_in if name not in shared]
    outs = {**outs, **{there: (inputs[name].shape, inputs[name].dtype) for name, there in shared.items()}}
    outs = {**outs, **{name: (kept[name].shape, kept[name].dtype) for name in held}}
    order = {name: PARTS.get(name, (0,)) if stage == "four" else (0,) for name in far_in}
    names_in, names_out = list(inputs), list(outs)
    aliases = {names_in.index(name) + 1: names_out.index(name) for name in held}

    def kernel(place_ref, *refs):
        given = dict(zip(inputs, refs))
        refs = refs[len(inputs) :]
        results = dict(zip(outs, refs))
        refs = refs[len(outs) :]
        in_here = {name: results[there] for name, there in shared.items()}
        in_here, refs = {**in_here, **dict(zip(own, refs))}, refs[len(own) :]
        out_here, refs = dict(zip(far, refs)), refs[len(far) :]
        in_sems, out_sems, *rest = refs
        place = 0
        for name in far_in:
            sems = in_sems.at[pl.ds(place, len(order[name]))]
            given[name] = Slot(given[name], in_here[name], sems, in_here[name], order[name])
            place += len(order[name])
        for place, name in enumerate(far):
            results[name] = Slot(out_here[name], results[name], out_sems.at[pl.ds(place, 1)], out_here[name])
        arrays, results = Inputs(given), Arrays({name: results[name] for name in made})
        arrays.start(first)
        body(dims, place_ref, arrays, results, *rest)
        arrays.wait()
        results.start()
        results.wait()

    def space(name):
        return pltpu.HBM if name in far_in or name in far else pltpu.VMEM

    buffers = [(inputs[name].shape, inputs[name].dtype) for name in own] + [outs[name] for name in far]
    sizes = [jnp.dtype(dtype).itemsize * math.prod(shape) for shape, dtype in [*buffers, *scratch]]
    results = pl.pallas_call(
        kernel,
        out_shape=[space(name)(shape, dtype) for name, (shape, dtype) in outs.items()],
        in_specs=[pl.BlockSpec(memory_space=pltpu.SMEM)]
        + [pl.BlockSpec(memory_space=space(name)) for name in inputs],
        out_specs=[pl.BlockSpec(memory_space=space(name)) for name in outs],
        input_output_aliases=aliases,
        scratch_shapes=[pltpu.VMEM(shape, dtype) for shape, dtype in buffers]
        + [pltpu.SemaphoreType.DMA((max(1, sum(map(len, order.values()))),)), pltpu.SemaphoreType.DMA((max(1, len(far)),))]
        + [pltpu.VMEM(shape, dtype) for shape, dtype in scratch],
        compiler_params=pltpu.CompilerParams(vmem_limit_bytes=sum(sizes) + SPARE.get(stage, 4) * MIB),
        cost_estimate=pl.CostEstimate(flops=FLOPS, bytes_accessed=0, transcendentals=0),
    )(
        kept["place"],
        *(pltpu.with_memory_space_constraint(value, space(name)) for name, value in inputs.items()),
    )
    results = dict(zip(outs, results))
    kept.update(results)
    return {name: results[name] for name in made}
SPARE = dict(five=7, middle=6, second=5)
MIB = 1 << 20
PARTS = dict(w5=(4, 3, 5, 1, 7, 0, 2, 6, 8))
FLOPS = 1000
TAPS_Q = 5


def counts(place_ref, crops):
    full, half = jnp.int32(0), jnp.int32(0)
    for crop in range(crops):
        rows, cols = place_ref[crop], place_ref[crops + crop]
        full += rows * cols
        half += ((rows + 1) >> 1) * ((cols + 1) >> 1)
    return full.astype(F32), half.astype(F32)


def one_hot(rows, columns, picked):
    row = lax.broadcasted_iota(jnp.int32, (rows, columns), 0)
    column = lax.broadcasted_iota(jnp.int32, (rows, columns), 1)
    return jnp.where(picked(row, column), 1.0, 0.0).astype(BF16)


def col_shift(pixels, map_cols, shift):
    edge = map_cols - 1 if shift > 0 else 0

    def picked(row, column):
        return (column == row + shift) & ((row & (map_cols - 1)) != edge)

    return one_hot(pixels, pixels, picked)


def to_phases(pixels, map_cols):
    quarter, half_cols = pixels // 4, map_cols // 2

    def picked(row, column):
        phase, place = row >> log2(quarter), row & (quarter - 1)
        map_row = 2 * (place >> log2(half_cols)) + (phase >> 1)
        map_col = 2 * (place & (half_cols - 1)) + (phase & 1)
        return column == map_row * map_cols + map_col

    return one_hot(pixels, pixels, picked)


def half_shift(pixels, crop_pixels, half_cols, row_shift, col_shift):
    def picked(row, column):
        place = row & (crop_pixels - 1)
        inside = column == row - row_shift * half_cols - col_shift
        if row_shift:
            inside &= place >= half_cols
        if col_shift:
            inside &= (place & (half_cols - 1)) != 0
        return inside

    return one_hot(pixels, pixels, picked)


class Dims:
    def __init__(self, crops, map_rows, map_cols, strips, cuts, widths):
        self.cuts = cuts
        self.crops, self.map_rows, self.map_cols, self.strips = crops, map_rows, map_cols, strips
        self.pixels = map_rows * map_cols
        self.half_pixels = self.pixels // 4
        self.full = crops * self.pixels
        self.half = crops * self.half_pixels
        self.strip = self.pixels // strips
        self.half_strip = self.half_pixels // strips
        self.padded = (map_rows + 2) * map_cols
        self.widths = widths
        self.starts = [sum(widths[:i]) for i in range(len(widths))]

    def cut(self, norm, step=0, count=1):
        size = self.widths[norm] // count
        return pl.ds(self.starts[norm] + step * size, size)


def moments(sums, squares, pixels, dims, norm, params_ref, stats_ref):
    span = dims.cut(norm)
    center = total(sums) / pixels
    scale = lax.rsqrt(total(squares) / pixels - center * center + EPSILON)
    stats_ref[0:1, span] = center
    stats_ref[1:2, span] = scale
    slope = scale * params_ref[0:1, :]
    return slope, params_ref[1:2, :] - center * slope


def affine(dims, norm, stats_ref, params_ref):
    span = dims.cut(norm)
    center, scale = stats_ref[0:1, span], stats_ref[1:2, span]
    slope = scale * params_ref[0:1, :]
    return center, scale, slope, params_ref[1:2, :] - center * slope


def tap_phase(tap):
    down, across = tap // 3, tap % 3
    return 2 * (down != 1) + (across != 1), (down == 0, across == 0)


SHIFTED = [tap for tap in range(9) if tap_phase(tap)[1] != (False, False)]


BEFORE, AFTER, PHASES, BACK_SHIFT, UNPHASED, FORE_SHIFT, HOTS = 0, 1, 2, 3, 6, 7, 10


def place_body(dims, place_ref, _, outs):
    full_mask, phase_mask, half_mask, hot = (
        outs[name] for name in ("full_mask", "phase_mask", "half_mask", "hot")
    )
    crops, pixels, half_pixels = dims.crops, dims.pixels, dims.half_pixels
    place = lax.broadcasted_iota(jnp.int32, (pixels, LANES), 0)
    half_place = lax.broadcasted_iota(jnp.int32, (half_pixels, LANES), 0)
    half_cols = dims.map_cols // 2
    for crop in range(crops):
        rows, cols = place_ref[crop], place_ref[crops + crop]
        inside = (place >> log2(dims.map_cols) < rows) & ((place & (dims.map_cols - 1)) < cols)
        full_mask[crop * pixels : (crop + 1) * pixels, :] = jnp.where(inside, 1.0, 0.0)
        for phase in range(4):
            map_row = 2 * (half_place >> log2(half_cols)) + (phase >> 1)
            map_col = 2 * (half_place & (half_cols - 1)) + (phase & 1)
            inside = jnp.where((map_row < rows) & (map_col < cols), 1.0, 0.0)
            start = phase * dims.half + crop * half_pixels
            phase_mask[start : start + half_pixels, :] = inside
            if phase == 0:
                half_mask[crop * half_pixels : (crop + 1) * half_pixels, :] = inside

    hot[BEFORE] = col_shift(pixels, dims.map_cols, -1)
    hot[AFTER] = col_shift(pixels, dims.map_cols, 1)
    hot[PHASES] = to_phases(pixels, dims.map_cols)
    for index, shift in enumerate(((0, 1), (1, 0), (1, 1))):
        hot[BACK_SHIFT + index] = half_shift(dims.half, half_pixels, half_cols, *shift)
        hot[FORE_SHIFT + index] = hot[BACK_SHIFT + index].T
    hot[UNPHASED] = hot[PHASES].T


def pieces(start, size, step):
    return [slice(begin, begin + step) for begin in range(start, start + size, step)]


def blank_frame(dims, framed, columns):
    blank = jnp.zeros((dims.map_cols, columns), BF16)
    for crop in range(dims.crops):
        framed[crop * dims.padded : crop * dims.padded + dims.map_cols, :] = blank
        framed[(crop + 1) * dims.padded - dims.map_cols : (crop + 1) * dims.padded, :] = blank


class Sums:
    def __init__(self, columns):
        self.columns = columns
        self.parts = {}

    def add(self, block, first, second):
        old = self.parts.get(block.start)
        new = fold(first), fold(second)
        self.parts[block.start] = new if old is None else (old[0] + new[0], old[1] + new[1])

    def get(self):
        parts = [self.parts[start] for start in sorted(self.parts)]
        return tuple(jnp.concatenate(values, axis=1) for values in zip(*parts))


ROWS = 32
BLOCK = 256
STRIPS = ("strip", "strip_core", "strips_chip", "strips_chip")


def first_body(dims, place_ref, ins, outs, z3, act, s1):
    strips = dims.strips
    xm, z1, a1, z2, a2, mid, stats_ref = (
        outs[name] for name in words("xm z1 a1 z2", "a2 mid stats").split()
    )
    crops, pixels, half_pixels = dims.crops, dims.pixels, dims.half_pixels
    full_count, half_count = counts(place_ref, crops)
    me = place_ref[2 * crops]
    full_mask = ins["full_mask"]

    for step in range(strips):
        strip = me ^ step
        for crop in range(crops):
            rows = pl.ds(pl.multiple_of(crop * pixels + strip * dims.strip, dims.strip), dims.strip)
            cells = ins[f"x{step}"][crop * dims.strip : (crop + 1) * dims.strip, :]
            xm[rows, :] = cells * wide(full_mask[rows, :].astype(BF16), cells.shape[1])
    ins.start()
    tiles = pieces(0, dims.full, pixels)

    w1 = ins["w1"]
    sums = Sums(dims.widths[0])
    for tile in tiles:
        zone = dot(xm[tile, :], w1[...])
        z1[tile, :] = zone
        sums.add(slice(0, dims.widths[0]), zone, zone * zone)
    slope, offset = moments(*sums.get(), full_count, dims, 0, ins["n1"], stats_ref)

    width = dims.widths[0]
    blank_frame(dims, s1, 3 * width)
    hot = ins["hot"]
    for crop, tile in enumerate(tiles):
        start = crop * dims.padded + dims.map_cols
        for rows, target in zip(pieces(tile.start, pixels, ROWS), pieces(start, pixels, ROWS)):
            cells = silu(z1[rows, :] * slope + offset) * wide(full_mask[rows, :], width)
            cells = cells.astype(BF16)
            a1[rows, :] = cells
            s1[target, width : 2 * width] = cells
        rows = slice(start, start + pixels)
        cells = s1[rows, width : 2 * width]
        s1[rows, :width] = dot(hot[BEFORE], cells).astype(BF16)
        s1[rows, 2 * width :] = dot(hot[AFTER], cells).astype(BF16)

    w2 = ins["w2"]
    sums = Sums(dims.widths[1])
    for crop, tile in enumerate(tiles):
        zone = 0.0
        for down in range(3):
            start = crop * dims.padded + down * dims.map_cols
            zone += dot(s1[start : start + pixels, :], w2[down * 3 * width : (down + 1) * 3 * width, :])
        z2[tile, :] = zone
        inside = zone * wide(full_mask[tile, :], zone.shape[1])
        sums.add(slice(0, dims.widths[1]), inside, inside * zone)
    slope, offset = moments(*sums.get(), full_count, dims, 1, ins["n2"], stats_ref)

    w3 = ins["w3"]
    sums = Sums(dims.widths[2])
    for tile in tiles:
        for rows in pieces(tile.start, pixels, ROWS):
            cells = silu(z2[rows, :] * slope + offset) * wide(full_mask[rows, :], dims.widths[1])
            a2[rows, :] = cells.astype(BF16)
        for block in pieces(0, dims.widths[2], BLOCK):
            zone = dot(a2[tile, :], w3[:, block])
            z3[tile, block] = zone
            outs["z3"][tile, block] = zone.astype(BF16)
            sums.add(block, zone, zone * zone)
    slope, offset = moments(*sums.get(), full_count, dims, 2, ins["n3"], stats_ref)

    for crop, tile in enumerate(tiles):
        here = act.at[crop & 1]
        for rows, target in zip(pieces(tile.start, pixels, 16), pieces(0, pixels, 16)):
            cells = xm[rows, :].astype(F32) + (z3[rows, :] * slope + offset)
            here[target, :] = (silu(cells) * wide(full_mask[rows, :], dims.widths[2])).astype(BF16)
        for block in pieces(0, dims.widths[2], BLOCK):
            cells = dot(hot[PHASES], here[:, block]).astype(BF16)
            for phase in range(4):
                start = phase * dims.half + crop * half_pixels
                part = cells[phase * half_pixels : (phase + 1) * half_pixels]
                mid[start : start + half_pixels, block] = part

    z4, a4, sh4, z5, a5 = (outs[name] for name in words("z4 a4 sh4 z5", "a5").split())
    phases = pieces(0, dims.full, dims.half)

    w4 = ins["w4"]
    width = dims.widths[3]
    sums = Sums(width)
    for tile in phases:
        for block in pieces(0, width, BLOCK):
            zone = dot(mid[tile, :], w4[:, block])
            z4[tile, block] = zone
            sums.add(block, zone, zone * zone)
    slope, offset = moments(*sums.get(), full_count, dims, 3, ins["n4"], stats_ref)
    phase_mask = ins["phase_mask"]
    for rows in pieces(0, dims.full, ROWS):
        cells = silu(z4[rows, :] * slope + offset) * wide(phase_mask[rows, :], width)
        a4[rows, :] = cells.astype(BF16)

    w5, half_mask = ins["w5"], ins["half_mask"]
    for place, tap in enumerate(SHIFTED):
        phase, (row_shift, col_shift_) = tap_phase(tap)
        picked = hot[BACK_SHIFT + 2 * row_shift + col_shift_ - 1]
        sh4[place * dims.half : (place + 1) * dims.half, :] = dot(picked, a4[phases[phase], :]).astype(BF16)
    sums = Sums(width)
    for block in pieces(0, dims.widths[4], BLOCK):
        zone = 0.0
        for tap in range(9):
            if tap in SHIFTED:
                place = SHIFTED.index(tap)
                cells = sh4[place * dims.half : (place + 1) * dims.half, :]
            else:
                cells = a4[phases[tap_phase(tap)[0]], :]
            zone += dot(cells, w5[tap * width : (tap + 1) * width, block])
        z5[:, block] = zone
        inside = zone * wide(half_mask[...], BLOCK)
        sums.add(block, inside, inside * zone)
    slope, offset = moments(*sums.get(), half_count, dims, 4, ins["n5"], stats_ref)
    for rows in pieces(0, dims.half, ROWS):
        cells = silu(z5[rows, :] * slope + offset) * wide(half_mask[rows, :], dims.widths[4])
        a5[rows, :] = cells.astype(BF16)


def second_body(dims, place_ref, ins, outs, grad, wide_out, zone6, zone7, back, turned):
    strips = dims.strips
    mid, a5, half_mask = ins["mid"], ins["a5"], ins["half_mask"]
    dz6, dz7, norm_grad = outs["dz6"], outs["dz7"], outs["norm67"]
    crops, half_pixels, size = dims.crops, dims.half_pixels, dims.half_strip
    _, half_count = counts(place_ref, crops)
    me = place_ref[2 * crops]
    turned[...] = mid[0 : dims.half, :].T
    for step in range(strips):
        strip = me ^ step
        for crop in range(crops):
            rows = pl.ds(pl.multiple_of(crop * half_pixels + strip * size, size), size)
            grad[rows, :] = ins[f"g{step}"][crop * size : (crop + 1) * size, :]

    width = dims.widths[5]
    half = width // 2
    core = me & 1
    weights = ((ins["v6"], ins["n6"]), (ins["v7"], ins["n7"]))
    jobs = [
        (target, which, step)
        for target, which in ((outs["keep7"], core), (outs["send7"], 1 - core))
        for step in range(half // BLOCK)
    ]

    def forward(index):
        target, which, step = jobs[index]
        columns = pl.ds(pl.multiple_of(which * half + step * BLOCK, BLOCK), BLOCK)
        norms = []
        for cells, zone_ref, (weight, params) in (
            (a5[...], zone6.at[index & 1], weights[0]),
            (mid[0 : dims.half, :], zone7.at[index & 1], weights[1]),
        ):
            zone = dot(cells, weight[:, columns])
            zone_ref[...] = zone
            center = total(fold(zone)) / half_count
            scale = lax.rsqrt(total(fold(zone * zone)) / half_count - center * center + EPSILON)
            slope = scale * params[0:1, columns]
            norms.append((center, scale, slope, params[1:2, columns] - center * slope))
        return columns, norms

    def backward(index, columns, norms):
        target, which, step = jobs[index]
        first, second = zone6.at[index & 1], zone7.at[index & 1]
        offset = norms[0][3] + norms[1][3]
        bias = first_sum = second_sum = 0.0
        for rows in pieces(0, dims.half, ROWS):
            mask = wide(half_mask[rows, :], BLOCK)
            value6, value7 = first[rows, :], second[rows, :]
            summed = value6 * norms[0][2] + value7 * norms[1][2] + offset
            gate = sigmoid(summed) * mask
            value = summed * gate
            wide_out[rows, columns] = value.astype(BF16)
            outer_grad = grad[rows, columns].astype(F32) * (gate + value * (1.0 - gate))
            back[rows, :] = outer_grad
            bias += fold(outer_grad)
            first_sum += fold(outer_grad * value6)
            second_sum += fold(outer_grad * value7)
        bias = total(bias)
        lines = []
        for place, products in enumerate((first_sum, second_sum)):
            center, scale, slope, _ = norms[place]
            gain = (total(products) - center * bias) * scale
            base = pl.multiple_of(place * width + which * half + step * BLOCK, BLOCK)
            norm_grad[0:1, pl.ds(base, BLOCK)] = gain
            norm_grad[1:2, pl.ds(base, BLOCK)] = bias
            tilt = scale * gain / half_count
            lines.append((slope, slope * (center * tilt - bias / half_count), slope * tilt))
        for rows in pieces(0, dims.half, ROWS):
            mask = wide(half_mask[rows, :], BLOCK)
            outer_grad = back[rows, :]
            for zone_ref, dz, (slope, level, tilt) in ((first, dz6, lines[0]), (second, dz7, lines[1])):
                values = outer_grad * slope + level - zone_ref[rows, :] * tilt
                dz[rows, columns] = (mask * values).astype(BF16)
        shard = dims.widths[2] // dims.cuts
        inner = slice(step * shard, (step + 1) * shard)
        right = dz7[:, columns]
        for rows in pieces(0, dims.widths[2], BLOCK):
            product = dot(turned[rows, :], right).astype(BF16)
            for part in pieces(0, BLOCK, shard):
                target[(rows.start + part.start) // shard, inner] = product[part]

    ready = forward(0)
    for index in range(len(jobs)):
        here = ready
        if index + 1 < len(jobs):
            ready = forward(index + 1)
        backward(index, *here)
        if index + 1 == len(jobs) // 2:
            outs.start("keep7")
    for step in range(strips):
        strip = me ^ step
        for crop in range(crops):
            rows = pl.ds(pl.multiple_of(crop * half_pixels + strip * size, size), size)
            start = (step % 2 * crops + crop) * size if step > 1 else crop * size
            outs[STRIPS[step]][start : start + size, :] = wide_out[rows, :]


def halves(product):
    half = product.shape[1] // 2
    return product[:, :half].astype(BF16), product[:, half:].astype(BF16)


def store_cuts(target, start, product, cuts):
    shard = product.shape[0] // cuts
    for cut in range(cuts):
        target[cut, start : start + shard] = product[cut * shard : (cut + 1) * shard]


def norm_back_lines(sums, params_ref, stats_ref, dims, norm, pixels, norm_grad, at=0):
    center, scale, slope, _ = affine(dims, norm, stats_ref, params_ref)
    bias = total(sums[0])
    gain = (total(sums[1]) - center * bias) * scale
    norm_grad[0:1, at : at + dims.widths[norm]] = gain
    norm_grad[1:2, at : at + dims.widths[norm]] = bias
    tilt = scale * gain / pixels
    return slope, slope * (center * tilt - bias / pixels), slope * tilt


def five_back_body(dims, place_ref, ins, outs):
    ins.start()
    dz5, norm_grad, dz6 = outs["dz5"], outs["norm5"], ins["dz6"]
    _, half_count = counts(place_ref, dims.crops)
    core = place_ref[2 * dims.crops] & 1
    turned = ins["a5"][...].T
    half6 = dims.widths[5] // 2
    columns = dims.widths[4] // 2
    shard6 = dims.widths[4] // dims.cuts
    blocks6 = half6 // columns
    for target, which in ((outs["keepp"], core), (outs["sendp"], 1 - core)):
        for block in range(blocks6):
            here = pl.ds(pl.multiple_of(which * half6 + block * columns, columns), columns)
            store_cuts(target, block * shard6, dot(turned, dz6[:, here]).astype(BF16), dims.cuts)

    width = dims.widths[4]
    z5, v6, half_mask = ins["z5"], ins["w6"], ins["half_mask"]
    _, _, slope, offset = affine(dims, 4, ins["stats"], ins["n5"])
    grads, sums = [], Sums(width)
    for block in pieces(0, width, BLOCK):
        zone = z5[:, block]
        grad = dot_nt(dz6[...], v6[block, :])
        grad = grad * silu_slope(zone * slope[:, block] + offset[:, block])
        sums.add(block, grad, grad * zone)
        grads.append(grad)
    line = norm_back_lines(sums.get(), ins["n5"], ins["stats"], dims, 4, half_count, norm_grad)
    for block, grad in zip(pieces(0, width, BLOCK), grads):
        values = grad * line[0][:, block] + line[1][:, block] - z5[:, block] * line[2][:, block]
        dz5[:, block] = (wide(half_mask[...], BLOCK) * values).astype(BF16)

    for block in pieces(0, dims.widths[2], BLOCK):
        outs["strided"][:, block] = dot_nt(ins["dz7"][...], ins["v7"][block, :])

    half = width // 2
    shard = width // dims.cuts
    a4, sh4 = ins["a4"], ins["sh4"]
    for stem, which in (("keep", core), ("send", 1 - core)):
        right = dz5[:, pl.ds(pl.multiple_of(which * half, half), half)]
        for tap in range(9):
            if tap in SHIFTED:
                start = SHIFTED.index(tap) * dims.half
                left = sh4[start : start + dims.half, :]
            else:
                start = tap_phase(tap)[0] * dims.half
                left = a4[start : start + dims.half, :]
            product = dot_tn(left, right).astype(BF16)
            if tap < TAPS_Q:
                store_cuts(outs[stem + "q"], tap * shard, product, dims.cuts)
            else:
                at = blocks6 * shard6 + (tap - TAPS_Q) * shard
                store_cuts(outs[stem + "p"], at, product, dims.cuts)
        if stem == "keep":
            outs.start()


def four_back_body(dims, place_ref, ins, outs, shifted, four_grad):
    ins.start()
    dz4, norm_grad = outs["dz4"], outs["norm4"]
    hot, dz5, z4, phase_mask = ins["hot"], ins["dz5"], ins["z4"], ins["phase_mask"]
    full_count, _ = counts(place_ref, dims.crops)
    width = dims.widths[3]
    for place in range(3):
        rows = slice(place * dims.half, (place + 1) * dims.half)
        shifted[rows, :] = dot(hot[FORE_SHIFT + place], dz5[...]).astype(BF16)
    _, _, slope, offset = affine(dims, 3, ins["stats"], ins["n4"])
    sums = Sums(width)
    for phase, tile in enumerate(pieces(0, dims.full, dims.half)):
        for block in pieces(0, width, BLOCK):
            grad = 0.0
            for tap in range(9):
                own, (row_shift, col_shift_) = tap_phase(tap)
                if own != phase:
                    continue
                if tap in SHIFTED:
                    start = (2 * row_shift + col_shift_ - 1) * dims.half
                    left = shifted[start : start + dims.half, :]
                else:
                    left = dz5[...]
                grad += dot_nt(left, ins.part("w5", tap)[block, :])
            zone = z4[tile, block]
            grad = grad * wide(phase_mask[tile, :], BLOCK)
            grad = grad * silu_slope(zone * slope[:, block] + offset[:, block])
            four_grad[tile, block] = grad
            sums.add(block, grad, grad * zone)
    line = norm_back_lines(sums.get(), ins["n4"], ins["stats"], dims, 3, full_count, norm_grad)
    for rows in pieces(0, dims.full, ROWS):
        values = four_grad[rows, :] * line[0] + line[1] - z4[rows, :] * line[2]
        dz4[rows, :] = (wide(phase_mask[rows, :], width) * values).astype(BF16)


def middle_back_body(dims, place_ref, ins, outs, phase_grad):
    ins.start()
    both, joined_grad, dz3, norm_grad = (outs[name] for name in ("both34", "joined", "dz3", "norm3"))
    dz4, v4, strided, mid, a2 = (ins[name] for name in ("dz4", "v4", "strided", "mid", "a2"))
    hot, z3, xm, full_mask = ins["hot"], ins["z3"], ins["xm"], ins["full_mask"]
    crops, pixels, half_pixels = dims.crops, dims.pixels, dims.half_pixels
    full_count, _ = counts(place_ref, crops)
    width = dims.widths[2]

    columns = both.shape[3]
    shard = dims.widths[2] // dims.cuts
    for rows in pieces(0, width, 2 * shard):
        for half, product in enumerate(halves(dot_tn(mid[:, rows], dz4[...]))):
            for cut, part in enumerate(pieces(0, 2 * shard, shard)):
                for place, block in enumerate(pieces(0, product.shape[1], columns)):
                    here = slice(place * shard, (place + 1) * shard)
                    both[half, rows.start // shard + cut, here] = product[part, block]

    for phase, tile in enumerate(pieces(0, dims.full, dims.half)):
        for block in pieces(0, width, BLOCK):
            grad = dot_nt(dz4[tile, :], v4[block, :])
            if phase == 0:
                grad += strided[:, block]
            phase_grad[tile, block] = grad.astype(BF16)

    _, _, slope, offset = affine(dims, 2, ins["stats"], ins["n3"])
    sums = Sums(width)
    for crop, tile in enumerate(pieces(0, dims.full, pixels)):
        for block in pieces(0, width, BLOCK):
            starts = [phase * dims.half + crop * half_pixels for phase in range(4)]
            cells = [phase_grad[start : start + half_pixels, block] for start in starts]
            joined_grad[tile, block] = dot(hot[UNPHASED], jnp.concatenate(cells, axis=0))
        for rows in pieces(tile.start, pixels, 16):
            zone = z3[rows, :].astype(F32)
            value = xm[rows, :].astype(F32) + (zone * slope + offset)
            grad = joined_grad[rows, :] * silu_slope(value)
            joined_grad[rows, :] = grad
            sums.add(slice(0, width), grad, grad * zone)
    line = norm_back_lines(sums.get(), ins["n3"], ins["stats"], dims, 2, full_count, norm_grad)
    for rows in pieces(0, dims.full, 16):
        values = joined_grad[rows, :] * line[0] + line[1] - z3[rows, :].astype(F32) * line[2]
        dz3[rows, :] = (wide(full_mask[rows, :], width) * values).astype(BF16)

    half = width // 2
    shard3 = dims.widths[1] // dims.cuts
    start3 = shard * (dims.widths[3] // 2 // columns)
    turned = a2[...].T
    for which in range(2):
        for wide_block in range(half // BLOCK):
            start = which * half + wide_block * BLOCK
            product = dot(turned, dz3[:, start : start + BLOCK]).astype(BF16)
            for place, block in enumerate(pieces(0, BLOCK, columns)):
                at = start3 + (wide_block * (BLOCK // columns) + place) * shard3
                store_cuts(both.at[which], at, product[:, block], dims.cuts)


def last_body(dims, place_ref, ins, outs, one_grad, inputs_grad, framed, dz1, norm21, s1, both):
    strips = dims.strips
    norm_grad = norm21
    crops, pixels = dims.crops, dims.pixels
    full_count, _ = counts(place_ref, crops)
    me = place_ref[2 * crops]
    width = dims.widths[0]
    dz3, v3, z2, full_mask, hot, v2, z1, v1, joined_grad = (
        ins[name] for name in words("dz3 v3 z2 full_mask", "hot v2 z1 v1", "joined").split()
    )
    tiles = pieces(0, dims.full, pixels)
    whole = slice(0, width)

    _, _, slope, offset = affine(dims, 1, ins["stats"], ins["n2"])
    sums = Sums(width)
    for tile in tiles:
        zone = z2[tile, :]
        grad = dot_nt(dz3[tile, :], v3[...])
        grad = grad * silu_slope(zone * slope + offset)
        one_grad[tile, :] = grad
        sums.add(whole, grad, grad * zone)
    line = norm_back_lines(sums.get(), ins["n2"], ins["stats"], dims, 1, full_count, norm_grad)
    blank_frame(dims, framed, 3 * width)
    for crop, tile in enumerate(tiles):
        start = crop * dims.padded + dims.map_cols
        for rows, target in zip(pieces(tile.start, pixels, ROWS), pieces(start, pixels, ROWS)):
            values = one_grad[rows, :] * line[0] + line[1] - z2[rows, :] * line[2]
            framed[target, whole.stop : 2 * width] = (wide(full_mask[rows, :], width) * values).astype(BF16)
        rows = slice(start, start + pixels)
        values = framed[rows, width : 2 * width]
        framed[rows, :width] = dot(hot[AFTER], values).astype(BF16)
        framed[rows, 2 * width :] = dot(hot[BEFORE], values).astype(BF16)

    _, _, slope, offset = affine(dims, 0, ins["stats"], ins["n1"])
    sums = Sums(width)
    for crop, tile in enumerate(tiles):
        grad = 0.0
        for tap in range(9):
            down, across = tap // 3, tap % 3
            start = crop * dims.padded + (2 - down) * dims.map_cols
            left = framed[start : start + pixels, across * width : (across + 1) * width]
            grad += dot_nt(left, v2[tap * width : (tap + 1) * width, :])
        zone = z1[tile, :]
        grad = grad * wide(full_mask[tile, :], width) * silu_slope(zone * slope + offset)
        one_grad[tile, :] = grad
        sums.add(whole, grad, grad * zone)
    line = norm_back_lines(sums.get(), ins["n1"], ins["stats"], dims, 0, full_count, norm_grad, width)
    for tile in tiles:
        for rows in pieces(tile.start, pixels, ROWS):
            values = one_grad[rows, :] * line[0] + line[1] - z1[rows, :] * line[2]
            dz1[rows, :] = (wide(full_mask[rows, :], width) * values).astype(BF16)
        for block in pieces(0, dims.widths[2], BLOCK):
            grad = dot_nt(dz1[tile, :], v1[block, :]) + joined_grad[tile, block]
            inputs_grad[tile, block] = grad.astype(BF16)
    for step in range(strips):
        strip = me ^ step
        for crop in range(crops):
            rows = pl.ds(pl.multiple_of(crop * pixels + strip * dims.strip, dims.strip), dims.strip)
            start = (step % 2 * crops + crop) * dims.strip if step > 1 else crop * dims.strip
            outs[STRIPS[step]][start : start + dims.strip, :] = inputs_grad[rows, :]
    first_weights(dims, place_ref, ins, outs, framed, dz1, norm21, s1, both)


def norm_rows(dims):
    rows = [
        (norm, kind, row)
        for norm, width in enumerate(dims.widths)
        for kind in range(2)
        for row in range(max(1, width // dims.cuts // LANES))
    ]
    middle = (len(rows) + 1) // 2
    return rows[:middle], rows[middle:]


NORM_ROWS = 16


def norm_source(dims, norm):
    places = [("norm21", 1), ("norm21", None), ("norm3", None), ("norm4", None), ("norm5", None)]
    name, behind = (places + [("norm67", None), ("norm67", 5)])[norm]
    return name, 0 if behind is None else dims.widths[behind]


def first_weights(dims, place_ref, ins, outs, framed, dz1, norm21, s1, both):
    a1, hot, xm = (ins[name] for name in "a1 hot xm".split())
    blank_frame(dims, s1, 3 * dims.widths[0])
    for crop, tile in enumerate(pieces(0, dims.full, dims.pixels)):
        start = crop * dims.padded + dims.map_cols
        for place, shift in enumerate((BEFORE, None, AFTER)):
            cells = a1[tile, :] if shift is None else dot(hot[shift], a1[tile, :]).astype(BF16)
            here = slice(place * dims.widths[0], (place + 1) * dims.widths[0])
            s1[start : start + dims.pixels, here] = cells
    start2 = ins["both34"].shape[2]
    both[:, :, :start2] = ins["both34"][...]
    width = dims.widths[0]
    shard2, shard1 = width // dims.cuts, dims.widths[2] // dims.cuts
    row = dims.map_cols
    span = dims.crops * dims.padded - 2 * row
    for down in range(3):
        left = s1[down * row : down * row + span, :]
        for half, product in enumerate(halves(dot_tn(left, framed[row : row + span, width : 2 * width]))):
            for across in range(3):
                at = start2 + (3 * down + across) * shard2
                store_cuts(both.at[half], at, product[across * width : (across + 1) * width], dims.cuts)
    start = start2 + 9 * shard2
    for rows in pieces(0, dims.cuts * shard1, 2 * shard1):
        for half, product in enumerate(halves(dot_tn(xm[:, rows], dz1[...]))):
            for cut, part in enumerate(pieces(0, 2 * shard1, shard1)):
                both[half, rows.start // shard1 + cut, start : start + shard1] = product[part]
    start += shard1
    for cut in range(dims.cuts):
        for half, rows in enumerate(norm_rows(dims)):
            lines = []
            for norm, kind, row in rows:
                name, at = norm_source(dims, norm)
                at += cut * dims.widths[norm] // dims.cuts // LANES * LANES + row * LANES
                source = norm21 if name == "norm21" else ins[name]
                lines.append(source[kind : kind + 1, at : at + LANES])
            lines.append(jnp.zeros((NORM_ROWS - len(lines), LANES), F32))
            both[half, cut, start:] = jnp.concatenate(lines, axis=0).astype(BF16)
    core = place_ref[2 * dims.crops] & 1
    for half in range(2):

        @pl.when(core == half)
        def _(half=half):
            outs["keep"][...] = both[half]
            middle = dims.cuts // 2
            outs["send0"][...] = both[1 - half, :middle]
            outs["send1"][...] = both[1 - half, middle:]


def place_call(dims, kept):
    size = dims.pixels
    outs = dict(
        full_mask=((dims.full, LANES), F32),
        phase_mask=((dims.full, LANES), F32),
        half_mask=((dims.half, LANES), F32),
        hot=((HOTS, size, size), BF16),
    )
    return flow("place", place_body, dims, kept, {}, outs)


def named(stem, values):
    return {f"{stem}{index}": value for index, value in enumerate(values)}


def pick(kept, names):
    return {name: kept[name] for name in names.split()}


def first_call(dims, x_blocks, kept):
    full, half, widths = dims.full, dims.half, dims.widths
    inputs = {**named("x", x_blocks), **pick(kept, words("w1 n1 w2 n2", "w3 n3 w4 n4", "w5 n5 w6 w7"))}
    outs = dict(
        xm=((full, widths[2]), BF16),
        z1=((full, widths[0]), F32),
        a1=((full, widths[0]), BF16),
        z2=((full, widths[1]), F32),
        a2=((full, widths[1]), BF16),
        z3=((full, widths[2]), BF16),
        mid=((full, widths[2]), BF16),
        stats=((2, sum(widths)), F32),
        z4=((full, widths[3]), F32),
        a4=((full, widths[3]), BF16),
        sh4=((len(SHIFTED) * half, widths[3]), BF16),
        z5=((half, widths[4]), F32),
        a5=((half, widths[4]), BF16),
    )
    scratch = [((full, widths[2]), F32), ((2, dims.pixels, widths[2]), BF16)]
    scratch.append(((dims.crops * dims.padded, 3 * widths[0]), BF16))
    return flow("first", first_body, dims, kept, inputs, outs, scratch, "w1", share="w6 w7")


def second_call(dims, g_blocks, kept):
    half, widths, cuts = dims.half, dims.widths, dims.cuts
    inputs = {**named("g", g_blocks), **pick(kept, "n6 n7")}
    weight = ((cuts, widths[2] // cuts * (widths[6] // 2 // BLOCK), BLOCK), BF16)
    outs = dict(
        keep7=weight,
        send7=weight,
        dz6=((half, widths[5]), BF16),
        dz7=((half, widths[6]), BF16),
        norm67=((2, 2 * widths[5]), F32),
    )
    strips = {name: ((half // dims.strips, widths[5]), BF16) for name in STRIPS[:2]}
    strips[STRIPS[2]] = ((half // dims.strips * 2, widths[5]), BF16)
    zone = ((2, half, BLOCK), F32)
    scratch = [((half, widths[5]), BF16)] * 2 + [zone, zone, ((half, BLOCK), F32), ((widths[2], half), BF16)]
    return flow("second", second_body, dims, kept, inputs, {**outs, **strips}, scratch)


def five_back(dims, kept):
    half, widths, cuts = dims.half, dims.widths, dims.cuts
    shard, columns = widths[3] // cuts, widths[4] // 2
    rows_p = widths[4] // cuts * (widths[5] // 2 // columns) + (9 - TAPS_Q) * shard
    outs = dict(
        keepp=((cuts, rows_p, columns), BF16),
        sendp=((cuts, rows_p, columns), BF16),
        keepq=((cuts, TAPS_Q * shard, columns), BF16),
        sendq=((cuts, TAPS_Q * shard, columns), BF16),
        strided=((half, widths[2]), F32),
        dz5=((half, widths[4]), BF16),
        norm5=((2, widths[4]), F32),
    )
    return flow("five", five_back_body, dims, kept, pick(kept, "n5 w6"), outs, (), "w6")


def four_back(dims, kept):
    half, full, widths = dims.half, dims.full, dims.widths
    outs = dict(
        dz4=((full, widths[3]), BF16),
        norm4=((2, widths[3]), F32),
    )
    scratch = [((3 * half, widths[4]), BF16), ((full, widths[3]), F32)]
    return flow("four", four_back_body, dims, kept, pick(kept, "n4 w5 w4"), outs, scratch, "w5 w4", "", "w4")


def rows_34(dims):
    columns = dims.widths[0] // 2
    four = dims.widths[2] // dims.cuts * (dims.widths[3] // 2 // columns)
    three = dims.widths[1] // dims.cuts * (dims.widths[2] // 2 // columns)
    return four, three


def middle_back(dims, kept):
    full, widths, cuts = dims.full, dims.widths, dims.cuts
    weight = ((2, cuts, sum(rows_34(dims)), widths[0] // 2), BF16)
    outs = dict(
        both34=weight,
        joined=((full, widths[2]), F32),
        dz3=((full, widths[2]), BF16),
        norm3=((2, widths[2]), F32),
    )
    scratch = [((full, widths[2]), BF16)]
    inputs = pick(kept, "n3 w3 w2 w1")
    return flow("middle", middle_back_body, dims, kept, inputs, outs, scratch, share="w3 w2 w1")


def last_back(dims, kept):
    full, widths, cuts = dims.full, dims.widths, dims.cuts
    strips = {name: ((full // dims.strips, widths[2]), BF16) for name in STRIPS[:2]}
    strips[STRIPS[2]] = ((full // dims.strips * 2, widths[2]), BF16)
    rows = sum(rows_34(dims)) + 9 * (widths[0] // cuts) + widths[2] // cuts + NORM_ROWS
    columns = widths[0] // 2
    outs = dict(
        keep=((cuts, rows, columns), BF16),
        send0=((cuts // 2, rows, columns), BF16),
        send1=((cuts // 2, rows, columns), BF16),
        **strips,
    )
    framed = ((dims.crops * dims.padded, 3 * widths[0]), BF16)
    scratch = [
        ((full, widths[0]), F32),
        ((full, widths[2]), BF16),
        framed,
        ((full, widths[0]), BF16),
        ((2, 2 * widths[0]), F32),
        framed,
        ((2, cuts, rows, columns), BF16),
    ]
    return flow("last", last_body, dims, kept, pick(kept, "n2 n1"), outs, scratch)


class Job:
    def __init__(self, arrays, outer, inner, bit):
        self.arrays, self.outer, self.inner, self.bit = arrays, outer, inner, bit
        count, self.rows, self.columns = arrays[0].shape
        assert count == 2 * outer * inner
        assert len(arrays) == 2 or (inner == 1 and outer % 2 == 0)
        self.shape = (outer * inner, self.rows, self.columns)

    def step(self):
        if self.rows % 16:
            return self.rows
        most = max(16, (1 << 13) // self.columns)
        return max(size for size in range(16, self.rows + 1, 16) if self.rows % size == 0 and size <= most)


def add_call(place, groups, here):
    def kernel(place_ref, *refs):
        count = sum(len(job.arrays) for group in groups for job in group)
        sources, targets = refs[:count], refs[count:]
        for number, group in enumerate(groups):
            start = 0
            for job in group:
                (first, *seconds), sources = sources[: len(job.arrays)], sources[len(job.arrays) :]
                rank, shift = job.bit
                own = (place_ref[rank] >> shift) & 1
                for target, bit in ((targets[2 * number], 1 - own), (targets[2 * number + 1], own)):
                    for index in range(job.outer * job.inner):
                        outer, inner = index // job.inner, index % job.inner
                        source = (2 * outer + bit) * job.inner + inner
                        piece = outer * len(seconds) // job.outer
                        offset = piece * 2 * job.outer * job.inner // len(seconds)
                        size = job.step()

                        def add(
                            at,
                            _,
                            source=source,
                            offset=offset,
                            target=target,
                            index=index,
                            first=first,
                            second=seconds[piece],
                            size=size,
                            start=start,
                        ):
                            here_ = pl.ds(pl.multiple_of(at * size, size), size)
                            there = pl.ds(pl.multiple_of(start + at * size, 16 if size % 16 == 0 else 1), size)
                            value = first[source, here_, :].astype(F32) + second[source - offset, here_, :].astype(F32)
                            target[index, there, :] = value.astype(BF16)
                            return 0

                        lax.fori_loop(0, job.rows // size, add, 0)
                start += job.rows

    arrays = [value for group in groups for job in group for value in job.arrays]
    shapes = [
        (group[0].outer * group[0].inner, sum(job.rows for job in group), group[0].columns) for group in groups
    ]
    results = pl.pallas_call(
        kernel,
        out_shape=[
            (pltpu.VMEM if here else jax.ShapeDtypeStruct)(shape, BF16) for shape in shapes for _ in range(2)
        ],
        in_specs=[pl.BlockSpec(memory_space=pltpu.SMEM)] + [pl.BlockSpec(memory_space=pltpu.VMEM)] * len(arrays),
        out_specs=[pl.BlockSpec(memory_space=pltpu.VMEM)] * (2 * len(shapes)),
        compiler_params=pltpu.CompilerParams(
            vmem_limit_bytes=(4 if here else 16) * sum(math.prod(shape) for shape in shapes) + 2 * MIB
        ),
        cost_estimate=pl.CostEstimate(flops=FLOPS, bytes_accessed=0, transcendentals=0),
    )(place, *(pltpu.with_memory_space_constraint(value, pltpu.VMEM) if here else value for value in arrays))
    return list(zip(results[::2], results[1::2]))


def finish_call(dims, place, images, image_at, own, other):
    shards = [width // images for width in dims.widths]
    columns = own.shape[1]
    count4, count3 = dims.widths[3] // 2 // columns, dims.widths[2] // 2 // columns
    outs = [
        (shards[2], dims.widths[3]),
        (shards[1], dims.widths[2]),
        (9 * shards[0], dims.widths[1]),
        (shards[2], dims.widths[0]),
        *((2, shard) for shard in shards),
    ]

    def kernel(place_ref, own_ref, other_ref, four, three, two, one, *norms):
        core = place_ref[image_at - 1] & 1
        image = place_ref[image_at]

        def put(halves):
            at = 0
            for target, shard, count in ((four, shards[2], count4), (three, shards[1], count3)):
                for half, values in enumerate(halves):
                    for block in range(count):
                        start = (half * count + block) * columns
                        rows = slice(at + block * shard, at + (block + 1) * shard)
                        target[:, start : start + columns] = values[rows, :].astype(F32)
                at += count * shard
            for target in (two, one):
                size = target.shape[0]
                for half, values in enumerate(halves):
                    here = slice(half * columns, (half + 1) * columns)
                    target[:, here] = values[at : at + size, :].astype(F32)
                at += size
            cut = image * dims.cuts // images
            for values, rows in zip(halves, norm_rows(dims)):
                lines = values[at : at + NORM_ROWS, :].astype(F32)
                for index, (norm, kind, row) in enumerate(rows):
                    shard = shards[norm]
                    if shard >= LANES:
                        norms[norm][kind : kind + 1, row * LANES : (row + 1) * LANES] = lines[index : index + 1]
                        continue
                    lane = image * shard - cut * (dims.widths[norm] // dims.cuts) // LANES * LANES - row * LANES

                    @pl.when((lane >= 0) & (lane < LANES))
                    def _(lane=lane, norm=norm, kind=kind, index=index, shard=shard):
                        line = pltpu.roll(lines[index // 8 * 8 : index // 8 * 8 + 8], LANES - lane, 1)
                        norms[norm][kind : kind + 1, :] = line[index % 8 : index % 8 + 1, :shard]

        @pl.when(core == 0)
        def _():
            put((own_ref, other_ref))

        @pl.when(core == 1)
        def _():
            put((other_ref, own_ref))

    return pl.pallas_call(
        kernel,
        out_shape=[jax.ShapeDtypeStruct(shape, F32) for shape in outs],
        in_specs=[pl.BlockSpec(memory_space=pltpu.SMEM)] + [pl.BlockSpec(memory_space=pltpu.VMEM)] * 2,
        out_specs=[pl.BlockSpec(memory_space=pltpu.VMEM)] * len(outs),
        compiler_params=pltpu.CompilerParams(vmem_limit_bytes=8 * MIB),
        cost_estimate=pl.CostEstimate(flops=FLOPS, bytes_accessed=0, transcendentals=0),
    )(place, own, other)


def stack_call(dims, place, blocks, whole=None):
    me_at = 2 * dims.crops
    steps = list(blocks)
    count = len(steps)
    shape = (count, *blocks[steps[0]].shape)

    def kernel(place_ref, *refs):
        sources = refs[:count]
        target, held, in_sems, out_sems = refs[-4:]
        me = place_ref[me_at]
        loads = [
            pltpu.make_async_copy(source, held.at[index], in_sems.at[index])
            for index, source in enumerate(sources)
        ]
        stores = [
            pltpu.make_async_copy(held.at[index], target.at[me ^ step], out_sems.at[index])
            for index, step in enumerate(steps)
        ]
        for load in loads:
            load.start()
        for load, store in zip(loads, stores):
            load.wait()
            store.start()
        for store in stores:
            store.wait()

    given = [] if whole is None else [whole]
    return pl.pallas_call(
        kernel,
        out_shape=pltpu.HBM((dims.strips, *shape[1:]), BF16),
        in_specs=[pl.BlockSpec(memory_space=pltpu.SMEM)]
        + [pl.BlockSpec(memory_space=pl.ANY)] * count
        + [pl.BlockSpec(memory_space=pltpu.HBM)] * len(given),
        out_specs=pl.BlockSpec(memory_space=pltpu.HBM),
        input_output_aliases={count + 1: 0} if given else {},
        scratch_shapes=[pltpu.VMEM(shape, BF16)] + [pltpu.SemaphoreType.DMA((count,))] * 2,
        compiler_params=pltpu.CompilerParams(vmem_limit_bytes=2 * math.prod(shape) + MIB),
        cost_estimate=pl.CostEstimate(flops=FLOPS, bytes_accessed=0, transcendentals=0),
    )(place, *blocks.values(), *given)


def partner(count, step):
    return [(i, i ^ step) for i in range(count)]


def swap(value, axis, step):
    return lax.ppermute(value, axis, partner(lax.axis_size(axis), step))


def after(value, *tokens):
    return lax.optimization_barrier((value, *tokens))[0]


def exchange(parts, order):
    moved = dict.fromkeys(range(len(parts)))
    moved[0] = parts[0]
    for step in order:
        moved[step] = swap(parts[step], "rows", step)
    return [moved[step] for step in range(len(parts))]


class Results:
    def __init__(self, turns, dims, place, strips):
        self.turns, self.dims, self.place = turns, dims, place
        self.own, self.core, chip = (strips[name] for name in STRIPS[:3])
        self.chip = swap(chip, "rows", 2)
        self.steps = [self.hand_on, self.stack]

    def advance(self):
        self.steps.pop(0)()

    def hand_on(self):
        chip, core = self.turns.take((self.chip, self.core))
        rows = self.own.shape[0]
        self.near, far = chip[:rows], chip[rows:]
        self.turns.done(far)
        self.parts = {0: self.own, 1: swap(core, "rows", 1), 2: self.near, 3: swap(far, "rows", 1)}

    def stack(self):
        self.whole = stack_call(self.dims, self.place, self.turns.take(self.parts))
        self.turns.done(self.whole)


def strips_of(strips, rank, steps):
    parts = []
    for step in steps:
        part = lax.dynamic_index_in_dim(strips, rank ^ step, 0, keepdims=False)
        parts.append(part.reshape(-1, part.shape[-1]))
    return parts


TAIL = words("7 p p 7", "c x c p", "7 p c 7", "x p b c", "c")


class Turns:
    def __init__(self):
        self.token = None

    def take(self, values):
        if self.token is None:
            return values
        return lax.optimization_barrier((values, self.token))[0]

    def done(self, token):
        self.token = token


class Reduction:
    def __init__(self, turns, place, rank_at, steps, keep, *sends):
        self.turns, self.place, self.rank_at = turns, place, rank_at
        self.left = sorted((step for axis, step in steps if axis == "images"), reverse=True)
        self.over_rows = any(axis == "rows" for axis, _ in steps)
        self.steps = [*steps, "rows", "core"]
        self.joining = []
        self.terms = (keep, *sends)

    def next_job(self):
        axis, distance = self.steps[0]
        arrays, inner = self.terms, 1
        if axis == "rows":
            count, rows, columns = arrays[0].shape
            arrays = [value.reshape(2 * count, rows // 2, columns) for value in arrays]
        else:
            inner = 1 << len([step for step in self.left if step < distance])
        outer = arrays[0].shape[0] // (2 * inner)
        return Job(arrays, outer, inner, (self.rank_at[axis], log2(distance)))

    def pass_on(self, send, kept):
        axis, distance = self.steps.pop(0)
        if axis == "images":
            self.left.remove(distance)
        self.terms = (kept, swap(send, axis, distance))

    def advance(self):
        if self.steps[0] == "rows":
            self.steps.pop(0)
            first, second = self.turns.take(self.terms)
            total = (first.astype(F32) + second.astype(F32)).astype(BF16)[0]
            self.turns.done(total)
            self.terms = (total, swap(total, "rows", 2))
        elif self.steps[0] == "core":
            self.steps.pop(0)
            total, other = self.turns.take(self.terms)
            if self.over_rows:
                bit = lax.axis_index("rows") >> 1
                total = jnp.concatenate(
                    [jnp.where(bit == 0, total, other), jnp.where(bit == 0, other, total)], axis=0
                )
            else:
                total = (total.astype(F32) + other.astype(F32)).astype(BF16)
            self.turns.done(total)
            self.terms = (total, swap(total, "rows", 1))
        else:
            others, self.joining = self.joining, []
            assert all(sorted(one.steps[:-2]) == sorted(self.steps[:-2]) for one in others)
            jobs = [one.next_job() for one in (self, *others)]
            given = self.turns.take([job.arrays for job in jobs])
            rank, shift = jobs[0].bit
            own = (self.place[rank] >> shift) & 1
            halves = []
            for bit in (1 - own, own):
                parts = []
                for job, arrays in zip(jobs, given):
                    sum_ = 0.0
                    for value in arrays:
                        value = value.reshape(job.outer, 2, job.inner, job.rows, job.columns)
                        sum_ += lax.dynamic_index_in_dim(value, bit, 1, keepdims=False).astype(F32)
                    parts.append(sum_.astype(BF16).reshape(job.shape))
                halves.append(parts[0] if len(parts) == 1 else jnp.concatenate(parts, axis=1))
            self.turns.done(halves[0])
            self.pass_on(*halves)

    def finish(self):
        assert not self.steps
        total, other = self.turns.take(self.terms)
        core = lax.axis_index("rows") & 1
        low = jnp.where(core == 0, total, other).astype(F32)
        high = jnp.where(core == 0, other, total).astype(F32)
        return low, high


def together(turns, place, *groups, here=True):
    jobs = [[one.next_job() for one in group] for group in groups]
    given = turns.take([[job.arrays for job in group] for group in jobs])
    for group, own in zip(jobs, given):
        for job, arrays in zip(group, own):
            job.arrays = arrays
    totals = add_call(place, jobs, here)
    turns.done(totals[-1][0])
    for group, (send, kept) in zip(groups, totals):
        assert all(one.left == group[0].left and one.steps == group[0].steps for one in group)
        group[0].pass_on(send, kept)


def by_image(value, cuts, images, shards, copied=0):
    if cuts == images:
        return value
    blocks, start = [], 0
    for shard in shards:
        block = value[:, start : start + shard].reshape(images, -1, value.shape[2])
        blocks.append(block)
        start += shard
    if copied:
        blocks.append(jnp.repeat(value[:, start:], images // cuts, axis=0))
    return jnp.concatenate(blocks, axis=1)


def local(features, crop_rows, crop_cols, *rest):
    out_grad = rest[-1]
    weights, norms = list(rest[0:-1:2]), rest[1:-1:2]
    rank = lax.axis_index("rows")
    strips, images = lax.axis_size("rows"), lax.axis_size("images")
    assert features.shape[0] == strips == 4
    _, crops, strip_rows, map_cols, _ = features.shape
    widths = [norm.shape[0] for norm in norms]
    cuts = min(images, min(widths) // 32)
    dims = Dims(crops, strip_rows * strips, map_cols, strips, cuts, widths)

    place = jnp.concatenate(
        [
            lax.dynamic_index_in_dim(crop_rows, rank, 0, keepdims=False),
            lax.dynamic_index_in_dim(crop_cols, rank, 0, keepdims=False),
            rank.astype(jnp.int32)[None],
            lax.axis_index("images").astype(jnp.int32)[None],
        ]
    )
    parts = strips_of(features, rank, range(strips))
    far_blocks = [swap(parts[step], "rows", step) for step in (2, 3)]
    x_blocks = [parts[0], swap(parts[1], "rows", 1), *far_blocks]
    kept = {"place": place}
    for index, (weight, norm) in enumerate(zip(weights, norms)):
        if weight.ndim == 3:
            weight = weight.transpose(1, 0, 2).reshape(-1, weight.shape[2])
        kept[f"w{index + 1}"] = weight
        kept[f"n{index + 1}"] = norm.T
    place_call(dims, kept)
    early = (*x_blocks, kept["hot"], kept["w2"], kept["w5"])
    g_parts = strips_of(out_grad, rank, range(strips))
    g_blocks = exchange(after(g_parts, *early), (2, 3, 1))

    distances = [1 << bit for bit in range((images - 1).bit_length())]
    near = [("images", step) for step in distances]
    across = [("rows", 2)]
    turns = Turns()

    rank_at = {"rows": 2 * crops, "images": 2 * crops + 1}

    def reduction(steps, shards, keep, send):
        keep, send = (by_image(value, cuts, images, shards) for value in (keep, send))
        return Reduction(turns, place, rank_at, steps, keep, swap(send, "rows", 1))

    shard = [width // images for width in widths]
    cut = [width // cuts for width in widths]
    first_call(dims, x_blocks, kept)
    wide = second_call(dims, g_blocks, kept)
    block_out = Results(turns, dims, place, wide)
    sum7 = reduction(near, [cut[2]] * (widths[6] // 2 // BLOCK), wide["keep7"], wide["send7"])
    turns.done(wide["norm67"])
    kept["dz6"] = turns.take(kept["dz6"])
    five = five_back(dims, kept)
    shards_p = [cut[4]] * (widths[5] // widths[4]) + [cut[3]] * (9 - TAPS_Q)
    sum_p = reduction(across + near, shards_p, five["keepp"], five["sendp"])
    sum_q = reduction(near[1:2] + near[:1] + near[2:], [cut[3]] * TAPS_Q, five["keepq"], five["sendq"])
    turns.done(five["norm5"])
    together(turns, place, [sum7])
    kept["dz5"] = turns.take(kept["dz5"])
    turns.done(four_back(dims, kept)["norm4"])
    together(turns, place, [sum_p], [sum_q])
    block_out.advance()
    kept["dz4"] = turns.take(kept["dz4"])
    middle = middle_back(dims, kept)
    turns.done(middle["norm3"])
    kept["dz3"] = turns.take(kept["dz3"])
    last = last_back(dims, kept)
    inputs_grad = Results(turns, dims, place, last)
    columns = widths[0] // 2
    shards_c = [cut[2]] * (widths[3] // 2 // columns) + [cut[1]] * (widths[2] // 2 // columns)
    shards_c += [cut[0]] * 9 + [cut[2]]
    keep = by_image(last["keep"], cuts, images, shards_c, NORM_ROWS)
    sends = [by_image(last[name], cuts // 2, images // 2, shards_c, NORM_ROWS) for name in ("send0", "send1")]
    sum_c = Reduction(turns, place, rank_at, near, keep, *(swap(send, "rows", 1) for send in sends))
    turns.done(last["keep"])
    for group in ([sum7], [sum_q], [sum_p], [sum_c]):
        together(turns, place, group, here=False)
    sum7.joining = [sum_q]

    def joined(halves, start=0, size=None):
        return jnp.concatenate([half[start : start + size] if size else half[start:] for half in halves], axis=1)

    def blocks(halves, start, shard, count):
        return jnp.concatenate(
            [half[start + block * shard : start + (block + 1) * shard] for half in halves for block in range(count)],
            axis=1,
        )

    count6 = widths[5] // widths[4]
    done = {}

    def finish(name):
        if name == "7":
            halves, count = sum7.finish(), widths[6] // 2 // BLOCK
            done["7"], done["5q"] = blocks(halves, 0, shard[2], count), joined(halves, shard[2] * count)
        elif name == "p":
            halves = sum_p.finish()
            done["6"], done["5p"] = blocks(halves, 0, shard[4], count6), joined(halves, shard[4] * count6)
        elif name == "c":
            own, other = turns.take(sum_c.terms)
            done["c"] = finish_call(dims, place, images, rank_at["images"], own, other)
        if "5" not in done and "5q" in done and "5p" in done:
            done["5"] = jnp.concatenate([done["5q"], done["5p"]], axis=0)
        turns.done([value for value in done.values()])

    sums = {"7": sum7, "p": sum_p, "c": sum_c, "x": inputs_grad, "b": block_out}
    names = TAIL.split()
    while len(done) < 6 or any(total.steps for total in sums.values()):
        for name in names:
            if sums[name].steps:
                sums[name].advance()
            elif {"p": "6"}.get(name, name) not in done and name in "7pc":
                finish(name)
        names = sums
    dw5 = done["5"].reshape(9, shard[3], widths[4]).transpose(1, 0, 2)
    dw4, dw3, dw2, dw1, *norm_grads = done["c"]
    dw2 = dw2.reshape(9, shard[0], widths[1]).transpose(1, 0, 2)
    norm_grads = [value.T for value in norm_grads]
    grads = [dw1, dw2, dw3, dw4, done["6"], done["7"]]
    grads.insert(4, dw5)
    results = [value for pair in zip(grads, norm_grads) for value in pair]
    block_out = block_out.whole.reshape(out_grad.shape)
    features_grad = inputs_grad.whole.reshape(features.shape)
    return (block_out, features_grad, *results)


def solution(mesh):
    strips = P(None, "images", "rows", None, None)
    grads = [P("images", None)] * 14
    grads[2] = grads[8] = P("images", None, None)
    return jax.shard_map(
        local,
        mesh=mesh,
        in_specs=(strips, P(None, "images"), P(None, "images")) + (P(),) * 14 + (strips,),
        out_specs=(strips, strips, *grads),
        check_vma=False,
    )
```

```python
import functools
import math

import jax
import jax.numpy as jnp
from jax import lax
from jax.experimental import pallas as pl
from jax.experimental.pallas import tpu as pltpu
from jax.sharding import PartitionSpec as P

EPSILON = 1e-05
LANES = 128
BF16, F32 = jnp.bfloat16, jnp.float32


def words(*parts):
    return " ".join(parts)


def names(**keys):
    return " ".join(keys)


def log2(size):
    assert size & (size - 1) == 0
    return size.bit_length() - 1


def dot(left, right):
    return jnp.dot(left, right, preferred_element_type=F32)


def dot_nt(left, right):
    return lax.dot_general(left, right, (((1,), (1,)), ((), ())), preferred_element_type=F32)


def dot_tn(left, right):
    return lax.dot_general(left, right, (((0,), (0,)), ((), ())), preferred_element_type=F32)


def sigmoid(values):
    return 0.5 * jnp.tanh(0.5 * values) + 0.5


def silu(values):
    return values * sigmoid(values)


def silu_slope(values):
    gate = sigmoid(values)
    return gate * (1.0 + values * (1.0 - gate))


def wide(mask, columns):
    return jnp.concatenate([mask] * (columns // LANES), axis=1)


def fold(values):
    rows, columns = values.shape
    return jnp.sum(values.reshape(rows // 8, 8, columns), axis=0)


def total(values):
    return jnp.sum(values, axis=0, keepdims=True)


class Slot:
    def __init__(self, source, target, semaphores, here, order=(0,)):
        size = here.shape[0] // len(order)
        self.copies, self.here, self.started = {}, here, False
        for part in order:
            rows = slice(part * size, (part + 1) * size)
            self.copies[part] = pltpu.make_async_copy(source.at[rows], target.at[rows], semaphores.at[part])

    def start(self):
        if not self.started:
            for copy in self.copies.values():
                copy.start()
        self.started = True

    def wait(self, part=None):
        self.start()
        for part in list(self.copies) if part is None else [part]:
            if part in self.copies:
                self.copies.pop(part).wait()


class Arrays:
    def __init__(self, arrays):
        self.arrays = arrays
        self.slots = {name: value for name, value in arrays.items() if isinstance(value, Slot)}

    def start(self, names=None):
        for name in self.slots if names is None else names.split():
            if name in self.slots:
                self.slots[name].start()

    def wait(self):
        for slot in self.slots.values():
            slot.wait()

    def __getitem__(self, name):
        return self.slots[name].here if name in self.slots else self.arrays[name]

    def __getattr__(self, name):
        return self[name]


class Inputs(Arrays):
    def part(self, name, part):
        slot = self.slots[name]
        size = slot.here.shape[0] // len(PARTS[name])
        slot.wait(part)
        return slot.here.at[part * size : (part + 1) * size]

    def __getitem__(self, name):
        if name in self.slots:
            self.slots[name].wait()
        return super().__getitem__(name)


READS = dict(
    place="",
    first=names(full_mask=0, hot=0, phase_mask=0, half_mask=0),
    second=names(mid=0, a5=0, v6=0, v7=0, half_mask=0),
    five=names(dz6=0, a5=0, half_mask=0, stats=0, z5=0, a4=0, sh4=0, dz7=0, v7=0),
    four=names(hot=0, dz5=0, stats=0, z4=0, phase_mask=0),
    middle=names(dz4=0, v4=0, strided=0, stats=0, hot=0, z3=0, xm=0, full_mask=0, mid=0, a2=0),
    last=names(dz3=0, v3=0, z2=0, v2=0, stats=0, full_mask=0, hot=0, z1=0, v1=0, joined=0, a1=0, xm=0, both34=0, norm67=0, norm5=0, norm4=0, norm3=0),
)
STAGES = list(READS)


def flow(stage, body, dims, kept, inputs, outs, scratch=(), first="", far="", share=""):
    far = far.split()
    later = " ".join(READS[name] for name in STAGES[STAGES.index(stage) + 1 :]).split()
    loaded = ["v" + name[1:] for name in share.split()]
    held = [name for name in kept if name in later and name not in loaded]
    read = {name: kept[name] for name in READS[stage].split()}
    inputs = {**inputs, **read, **{name: kept[name] for name in held}}
    far_in = [name for name in inputs if name[0] == "w"]
    made = dict(outs)
    shared = {name: "v" + name[1:] for name in share.split()}
    own = [name for name in far_in if name not in shared]
    outs = {**outs, **{there: (inputs[name].shape, inputs[name].dtype) for name, there in shared.items()}}
    outs = {**outs, **{name: (kept[name].shape, kept[name].dtype) for name in held}}
    order = {name: PARTS.get(name, (0,)) if stage == "four" else (0,) for name in far_in}
    names_in, names_out = list(inputs), list(outs)
    aliases = {names_in.index(name) + 1: names_out.index(name) for name in held}

    def kernel(place_ref, *refs):
        given = dict(zip(inputs, refs))
        refs = refs[len(inputs) :]
        results = dict(zip(outs, refs))
        refs = refs[len(outs) :]
        in_here = {name: results[there] for name, there in shared.items()}
        in_here, refs = {**in_here, **dict(zip(own, refs))}, refs[len(own) :]
        out_here, refs = dict(zip(far, refs)), refs[len(far) :]
        in_sems, out_sems, *rest = refs
        place = 0
        for name in far_in:
            sems = in_sems.at[pl.ds(place, len(order[name]))]
            given[name] = Slot(given[name], in_here[name], sems, in_here[name], order[name])
            place += len(order[name])
        for place, name in enumerate(far):
            results[name] = Slot(out_here[name], results[name], out_sems.at[pl.ds(place, 1)], out_here[name])
        arrays, results = Inputs(given), Arrays({name: results[name] for name in made})
        arrays.start(first)
        body(dims, place_ref, arrays, results, *rest)
        arrays.wait()
        results.start()
        results.wait()

    def space(name):
        return pltpu.HBM if name in far_in or name in far else pltpu.VMEM

    buffers = [(inputs[name].shape, inputs[name].dtype) for name in own] + [outs[name] for name in far]
    sizes = [jnp.dtype(dtype).itemsize * math.prod(shape) for shape, dtype in [*buffers, *scratch]]
    results = pl.pallas_call(
        kernel,
        out_shape=[space(name)(shape, dtype) for name, (shape, dtype) in outs.items()],
        in_specs=[pl.BlockSpec(memory_space=pltpu.SMEM)]
        + [pl.BlockSpec(memory_space=space(name)) for name in inputs],
        out_specs=[pl.BlockSpec(memory_space=space(name)) for name in outs],
        input_output_aliases=aliases,
        scratch_shapes=[pltpu.VMEM(shape, dtype) for shape, dtype in buffers]
        + [pltpu.SemaphoreType.DMA((max(1, sum(map(len, order.values()))),)), pltpu.SemaphoreType.DMA((max(1, len(far)),))]
        + [pltpu.VMEM(shape, dtype) for shape, dtype in scratch],
        compiler_params=pltpu.CompilerParams(vmem_limit_bytes=sum(sizes) + SPARE.get(stage, 4) * MIB),
        cost_estimate=pl.CostEstimate(flops=FLOPS, bytes_accessed=0, transcendentals=0),
    )(
        kept["place"],
        *(pltpu.with_memory_space_constraint(value, space(name)) for name, value in inputs.items()),
    )
    results = dict(zip(outs, results))
    kept.update(results)
    return {name: results[name] for name in made}
SPARE = dict(five=7, middle=6, second=5)
MIB = 1 << 20
PARTS = dict(w5=(4, 3, 5, 1, 7, 0, 2, 6, 8))
FLOPS = 1000
TAPS_Q = 5


def counts(place_ref, crops):
    full, half = jnp.int32(0), jnp.int32(0)
    for crop in range(crops):
        rows, cols = place_ref[crop], place_ref[crops + crop]
        full += rows * cols
        half += ((rows + 1) >> 1) * ((cols + 1) >> 1)
    return full.astype(F32), half.astype(F32)


def one_hot(rows, columns, picked):
    row = lax.broadcasted_iota(jnp.int32, (rows, columns), 0)
    column = lax.broadcasted_iota(jnp.int32, (rows, columns), 1)
    return jnp.where(picked(row, column), 1.0, 0.0).astype(BF16)


def col_shift(pixels, map_cols, shift):
    edge = map_cols - 1 if shift > 0 else 0

    def picked(row, column):
        return (column == row + shift) & ((row & (map_cols - 1)) != edge)

    return one_hot(pixels, pixels, picked)


def to_phases(pixels, map_cols):
    quarter, half_cols = pixels // 4, map_cols // 2

    def picked(row, column):
        phase, place = row >> log2(quarter), row & (quarter - 1)
        map_row = 2 * (place >> log2(half_cols)) + (phase >> 1)
        map_col = 2 * (place & (half_cols - 1)) + (phase & 1)
        return column == map_row * map_cols + map_col

    return one_hot(pixels, pixels, picked)


def half_shift(pixels, crop_pixels, half_cols, row_shift, col_shift):
    def picked(row, column):
        place = row & (crop_pixels - 1)
        inside = column == row - row_shift * half_cols - col_shift
        if row_shift:
            inside &= place >= half_cols
        if col_shift:
            inside &= (place & (half_cols - 1)) != 0
        return inside

    return one_hot(pixels, pixels, picked)


class Dims:
    def __init__(self, crops, map_rows, map_cols, strips, cuts, widths):
        self.cuts = cuts
        self.crops, self.map_rows, self.map_cols, self.strips = crops, map_rows, map_cols, strips
        self.pixels = map_rows * map_cols
        self.half_pixels = self.pixels // 4
        self.full = crops * self.pixels
        self.half = crops * self.half_pixels
        self.strip = self.pixels // strips
        self.half_strip = self.half_pixels // strips
        self.padded = (map_rows + 2) * map_cols
        self.widths = widths
        self.starts = [sum(widths[:i]) for i in range(len(widths))]

    def cut(self, norm, step=0, count=1):
        size = self.widths[norm] // count
        return pl.ds(self.starts[norm] + step * size, size)


def moments(sums, squares, pixels, dims, norm, params_ref, stats_ref):
    span = dims.cut(norm)
    center = total(sums) / pixels
    scale = lax.rsqrt(total(squares) / pixels - center * center + EPSILON)
    stats_ref[0:1, span] = center
    stats_ref[1:2, span] = scale
    slope = scale * params_ref[0:1, :]
    return slope, params_ref[1:2, :] - center * slope


def affine(dims, norm, stats_ref, params_ref):
    span = dims.cut(norm)
    center, scale = stats_ref[0:1, span], stats_ref[1:2, span]
    slope = scale * params_ref[0:1, :]
    return center, scale, slope, params_ref[1:2, :] - center * slope


def tap_phase(tap):
    down, across = tap // 3, tap % 3
    return 2 * (down != 1) + (across != 1), (down == 0, across == 0)


SHIFTED = [tap for tap in range(9) if tap_phase(tap)[1] != (False, False)]


BEFORE, AFTER, PHASES, BACK_SHIFT, UNPHASED, FORE_SHIFT, HOTS = 0, 1, 2, 3, 6, 7, 10


def place_body(dims, place_ref, _, outs):
    full_mask, phase_mask, half_mask, hot = (
        outs[name] for name in ("full_mask", "phase_mask", "half_mask", "hot")
    )
    crops, pixels, half_pixels = dims.crops, dims.pixels, dims.half_pixels
    place = lax.broadcasted_iota(jnp.int32, (pixels, LANES), 0)
    half_place = lax.broadcasted_iota(jnp.int32, (half_pixels, LANES), 0)
    half_cols = dims.map_cols // 2
    for crop in range(crops):
        rows, cols = place_ref[crop], place_ref[crops + crop]
        inside = (place >> log2(dims.map_cols) < rows) & ((place & (dims.map_cols - 1)) < cols)
        full_mask[crop * pixels : (crop + 1) * pixels, :] = jnp.where(inside, 1.0, 0.0)
        for phase in range(4):
            map_row = 2 * (half_place >> log2(half_cols)) + (phase >> 1)
            map_col = 2 * (half_place & (half_cols - 1)) + (phase & 1)
            inside = jnp.where((map_row < rows) & (map_col < cols), 1.0, 0.0)
            start = phase * dims.half + crop * half_pixels
            phase_mask[start : start + half_pixels, :] = inside
            if phase == 0:
                half_mask[crop * half_pixels : (crop + 1) * half_pixels, :] = inside

    hot[BEFORE] = col_shift(pixels, dims.map_cols, -1)
    hot[AFTER] = col_shift(pixels, dims.map_cols, 1)
    hot[PHASES] = to_phases(pixels, dims.map_cols)
    for index, shift in enumerate(((0, 1), (1, 0), (1, 1))):
        hot[BACK_SHIFT + index] = half_shift(dims.half, half_pixels, half_cols, *shift)
        hot[FORE_SHIFT + index] = hot[BACK_SHIFT + index].T
    hot[UNPHASED] = hot[PHASES].T


def pieces(start, size, step):
    return [slice(begin, begin + step) for begin in range(start, start + size, step)]


def blank_frame(dims, framed, columns):
    blank = jnp.zeros((dims.map_cols, columns), BF16)
    for crop in range(dims.crops):
        framed[crop * dims.padded : crop * dims.padded + dims.map_cols, :] = blank
        framed[(crop + 1) * dims.padded - dims.map_cols : (crop + 1) * dims.padded, :] = blank


class Sums:
    def __init__(self, columns):
        self.columns = columns
        self.parts = {}

    def add(self, block, first, second):
        old = self.parts.get(block.start)
        new = fold(first), fold(second)
        self.parts[block.start] = new if old is None else (old[0] + new[0], old[1] + new[1])

    def get(self):
        parts = [self.parts[start] for start in sorted(self.parts)]
        return tuple(jnp.concatenate(values, axis=1) for values in zip(*parts))


ROWS = 32
BLOCK = 256
STRIPS = ("strip", "strip_core", "strips_chip", "strips_chip")


def first_body(dims, place_ref, ins, outs, z3, act, s1):
    strips = dims.strips
    xm, z1, a1, z2, a2, mid, stats_ref = (
        outs[name] for name in names(xm=0, z1=0, a1=0, z2=0, a2=0, mid=0, stats=0).split()
    )
    crops, pixels, half_pixels = dims.crops, dims.pixels, dims.half_pixels
    full_count, half_count = counts(place_ref, crops)
    me = place_ref[2 * crops]
    full_mask = ins.full_mask

    for step in range(strips):
        strip = me ^ step
        for crop in range(crops):
            rows = pl.ds(pl.multiple_of(crop * pixels + strip * dims.strip, dims.strip), dims.strip)
            cells = ins[f"x{step}"][crop * dims.strip : (crop + 1) * dims.strip, :]
            xm[rows, :] = cells * wide(full_mask[rows, :].astype(BF16), cells.shape[1])
    ins.start()
    tiles = pieces(0, dims.full, pixels)

    w1 = ins.w1
    sums = Sums(dims.widths[0])
    for tile in tiles:
        zone = dot(xm[tile, :], w1[...])
        z1[tile, :] = zone
        sums.add(slice(0, dims.widths[0]), zone, zone * zone)
    slope, offset = moments(*sums.get(), full_count, dims, 0, ins.n1, stats_ref)

    width = dims.widths[0]
    blank_frame(dims, s1, 3 * width)
    hot = ins.hot
    for crop, tile in enumerate(tiles):
        start = crop * dims.padded + dims.map_cols
        for rows, target in zip(pieces(tile.start, pixels, ROWS), pieces(start, pixels, ROWS)):
            cells = silu(z1[rows, :] * slope + offset) * wide(full_mask[rows, :], width)
            cells = cells.astype(BF16)
            a1[rows, :] = cells
            s1[target, width : 2 * width] = cells
        rows = slice(start, start + pixels)
        cells = s1[rows, width : 2 * width]
        s1[rows, :width] = dot(hot[BEFORE], cells).astype(BF16)
        s1[rows, 2 * width :] = dot(hot[AFTER], cells).astype(BF16)

    w2 = ins.w2
    sums = Sums(dims.widths[1])
    for crop, tile in enumerate(tiles):
        zone = 0.0
        for down in range(3):
            start = crop * dims.padded + down * dims.map_cols
            zone += dot(s1[start : start + pixels, :], w2[down * 3 * width : (down + 1) * 3 * width, :])
        z2[tile, :] = zone
        inside = zone * wide(full_mask[tile, :], zone.shape[1])
        sums.add(slice(0, dims.widths[1]), inside, inside * zone)
    slope, offset = moments(*sums.get(), full_count, dims, 1, ins.n2, stats_ref)

    w3 = ins.w3
    sums = Sums(dims.widths[2])
    for tile in tiles:
        for rows in pieces(tile.start, pixels, ROWS):
            cells = silu(z2[rows, :] * slope + offset) * wide(full_mask[rows, :], dims.widths[1])
            a2[rows, :] = cells.astype(BF16)
        for block in pieces(0, dims.widths[2], BLOCK):
            zone = dot(a2[tile, :], w3[:, block])
            z3[tile, block] = zone
            outs.z3[tile, block] = zone.astype(BF16)
            sums.add(block, zone, zone * zone)
    slope, offset = moments(*sums.get(), full_count, dims, 2, ins.n3, stats_ref)

    for crop, tile in enumerate(tiles):
        here = act.at[crop & 1]
        for rows, target in zip(pieces(tile.start, pixels, 16), pieces(0, pixels, 16)):
            cells = xm[rows, :].astype(F32) + (z3[rows, :] * slope + offset)
            here[target, :] = (silu(cells) * wide(full_mask[rows, :], dims.widths[2])).astype(BF16)
        for block in pieces(0, dims.widths[2], BLOCK):
            cells = dot(hot[PHASES], here[:, block]).astype(BF16)
            for phase in range(4):
                start = phase * dims.half + crop * half_pixels
                part = cells[phase * half_pixels : (phase + 1) * half_pixels]
                mid[start : start + half_pixels, block] = part

    z4, a4, sh4, z5, a5 = (outs[name] for name in names(z4=0, a4=0, sh4=0, z5=0, a5=0).split())
    phases = pieces(0, dims.full, dims.half)

    w4 = ins.w4
    width = dims.widths[3]
    sums = Sums(width)
    for tile in phases:
        for block in pieces(0, width, BLOCK):
            zone = dot(mid[tile, :], w4[:, block])
            z4[tile, block] = zone
            sums.add(block, zone, zone * zone)
    slope, offset = moments(*sums.get(), full_count, dims, 3, ins.n4, stats_ref)
    phase_mask = ins.phase_mask
    for rows in pieces(0, dims.full, ROWS):
        cells = silu(z4[rows, :] * slope + offset) * wide(phase_mask[rows, :], width)
        a4[rows, :] = cells.astype(BF16)

    w5, half_mask = ins.w5, ins.half_mask
    for place, tap in enumerate(SHIFTED):
        phase, (row_shift, col_shift_) = tap_phase(tap)
        picked = hot[BACK_SHIFT + 2 * row_shift + col_shift_ - 1]
        sh4[place * dims.half : (place + 1) * dims.half, :] = dot(picked, a4[phases[phase], :]).astype(BF16)
    sums = Sums(width)
    for block in pieces(0, dims.widths[4], BLOCK):
        zone = 0.0
        for tap in range(9):
            if tap in SHIFTED:
                place = SHIFTED.index(tap)
                cells = sh4[place * dims.half : (place + 1) * dims.half, :]
            else:
                cells = a4[phases[tap_phase(tap)[0]], :]
            zone += dot(cells, w5[tap * width : (tap + 1) * width, block])
        z5[:, block] = zone
        inside = zone * wide(half_mask[...], BLOCK)
        sums.add(block, inside, inside * zone)
    slope, offset = moments(*sums.get(), half_count, dims, 4, ins.n5, stats_ref)
    for rows in pieces(0, dims.half, ROWS):
        cells = silu(z5[rows, :] * slope + offset) * wide(half_mask[rows, :], dims.widths[4])
        a5[rows, :] = cells.astype(BF16)


def second_body(dims, place_ref, ins, outs, grad, wide_out, zone6, zone7, back, turned):
    strips = dims.strips
    mid, a5, half_mask = ins.mid, ins.a5, ins.half_mask
    dz6, dz7, norm_grad = outs.dz6, outs.dz7, outs.norm67
    crops, half_pixels, size = dims.crops, dims.half_pixels, dims.half_strip
    _, half_count = counts(place_ref, crops)
    me = place_ref[2 * crops]
    turned[...] = mid[0 : dims.half, :].T
    for step in range(strips):
        strip = me ^ step
        for crop in range(crops):
            rows = pl.ds(pl.multiple_of(crop * half_pixels + strip * size, size), size)
            grad[rows, :] = ins[f"g{step}"][crop * size : (crop + 1) * size, :]

    width = dims.widths[5]
    half = width // 2
    core = me & 1
    weights = ((ins.v6, ins.n6), (ins.v7, ins.n7))
    jobs = [
        (target, which, step)
        for target, which in ((outs.keep7, core), (outs.send7, 1 - core))
        for step in range(half // BLOCK)
    ]

    def forward(index):
        target, which, step = jobs[index]
        columns = pl.ds(pl.multiple_of(which * half + step * BLOCK, BLOCK), BLOCK)
        norms = []
        for cells, zone_ref, (weight, params) in (
            (a5[...], zone6.at[index & 1], weights[0]),
            (mid[0 : dims.half, :], zone7.at[index & 1], weights[1]),
        ):
            zone = dot(cells, weight[:, columns])
            zone_ref[...] = zone
            center = total(fold(zone)) / half_count
            scale = lax.rsqrt(total(fold(zone * zone)) / half_count - center * center + EPSILON)
            slope = scale * params[0:1, columns]
            norms.append((center, scale, slope, params[1:2, columns] - center * slope))
        return columns, norms

    def backward(index, columns, norms):
        target, which, step = jobs[index]
        first, second = zone6.at[index & 1], zone7.at[index & 1]
        offset = norms[0][3] + norms[1][3]
        bias = first_sum = second_sum = 0.0
        for rows in pieces(0, dims.half, ROWS):
            mask = wide(half_mask[rows, :], BLOCK)
            value6, value7 = first[rows, :], second[rows, :]
            summed = value6 * norms[0][2] + value7 * norms[1][2] + offset
            gate = sigmoid(summed) * mask
            value = summed * gate
            wide_out[rows, columns] = value.astype(BF16)
            outer_grad = grad[rows, columns].astype(F32) * (gate + value * (1.0 - gate))
            back[rows, :] = outer_grad
            bias += fold(outer_grad)
            first_sum += fold(outer_grad * value6)
            second_sum += fold(outer_grad * value7)
        bias = total(bias)
        lines = []
        for place, products in enumerate((first_sum, second_sum)):
            center, scale, slope, _ = norms[place]
            gain = (total(products) - center * bias) * scale
            base = pl.multiple_of(place * width + which * half + step * BLOCK, BLOCK)
            norm_grad[0:1, pl.ds(base, BLOCK)] = gain
            norm_grad[1:2, pl.ds(base, BLOCK)] = bias
            tilt = scale * gain / half_count
            lines.append((slope, slope * (center * tilt - bias / half_count), slope * tilt))
        for rows in pieces(0, dims.half, ROWS):
            mask = wide(half_mask[rows, :], BLOCK)
            outer_grad = back[rows, :]
            for zone_ref, dz, (slope, level, tilt) in ((first, dz6, lines[0]), (second, dz7, lines[1])):
                values = outer_grad * slope + level - zone_ref[rows, :] * tilt
                dz[rows, columns] = (mask * values).astype(BF16)
        shard = dims.widths[2] // dims.cuts
        inner = slice(step * shard, (step + 1) * shard)
        right = dz7[:, columns]
        for rows in pieces(0, dims.widths[2], BLOCK):
            product = dot(turned[rows, :], right).astype(BF16)
            for part in pieces(0, BLOCK, shard):
                target[(rows.start + part.start) // shard, inner] = product[part]

    ready = forward(0)
    for index in range(len(jobs)):
        here = ready
        if index + 1 < len(jobs):
            ready = forward(index + 1)
        backward(index, *here)
        if index + 1 == len(jobs) // 2:
            outs.start("keep7")
    for step in range(strips):
        strip = me ^ step
        for crop in range(crops):
            rows = pl.ds(pl.multiple_of(crop * half_pixels + strip * size, size), size)
            start = (step % 2 * crops + crop) * size if step > 1 else crop * size
            outs[STRIPS[step]][start : start + size, :] = wide_out[rows, :]


def halves(product):
    half = product.shape[1] // 2
    return product[:, :half].astype(BF16), product[:, half:].astype(BF16)


def store_cuts(target, start, product, cuts):
    shard = product.shape[0] // cuts
    for cut in range(cuts):
        target[cut, start : start + shard] = product[cut * shard : (cut + 1) * shard]


def norm_back_lines(sums, params_ref, stats_ref, dims, norm, pixels, norm_grad, at=0):
    center, scale, slope, _ = affine(dims, norm, stats_ref, params_ref)
    bias = total(sums[0])
    gain = (total(sums[1]) - center * bias) * scale
    norm_grad[0:1, at : at + dims.widths[norm]] = gain
    norm_grad[1:2, at : at + dims.widths[norm]] = bias
    tilt = scale * gain / pixels
    return slope, slope * (center * tilt - bias / pixels), slope * tilt


def five_back_body(dims, place_ref, ins, outs):
    ins.start()
    dz5, norm_grad, dz6 = outs.dz5, outs.norm5, ins.dz6
    _, half_count = counts(place_ref, dims.crops)
    core = place_ref[2 * dims.crops] & 1
    turned = ins.a5[...].T
    half6 = dims.widths[5] // 2
    columns = dims.widths[4] // 2
    shard6 = dims.widths[4] // dims.cuts
    blocks6 = half6 // columns
    for target, which in ((outs.keepp, core), (outs.sendp, 1 - core)):
        for block in range(blocks6):
            here = pl.ds(pl.multiple_of(which * half6 + block * columns, columns), columns)
            store_cuts(target, block * shard6, dot(turned, dz6[:, here]).astype(BF16), dims.cuts)

    width = dims.widths[4]
    z5, v6, half_mask = ins.z5, ins.w6, ins.half_mask
    _, _, slope, offset = affine(dims, 4, ins.stats, ins.n5)
    grads, sums = [], Sums(width)
    for block in pieces(0, width, BLOCK):
        zone = z5[:, block]
        grad = dot_nt(dz6[...], v6[block, :])
        grad = grad * silu_slope(zone * slope[:, block] + offset[:, block])
        sums.add(block, grad, grad * zone)
        grads.append(grad)
    line = norm_back_lines(sums.get(), ins.n5, ins.stats, dims, 4, half_count, norm_grad)
    for block, grad in zip(pieces(0, width, BLOCK), grads):
        values = grad * line[0][:, block] + line[1][:, block] - z5[:, block] * line[2][:, block]
        dz5[:, block] = (wide(half_mask[...], BLOCK) * values).astype(BF16)

    for block in pieces(0, dims.widths[2], BLOCK):
        outs.strided[:, block] = dot_nt(ins.dz7[...], ins.v7[block, :])

    half = width // 2
    shard = width // dims.cuts
    a4, sh4 = ins.a4, ins.sh4
    for stem, which in (("keep", core), ("send", 1 - core)):
        right = dz5[:, pl.ds(pl.multiple_of(which * half, half), half)]
        for tap in range(9):
            if tap in SHIFTED:
                start = SHIFTED.index(tap) * dims.half
                left = sh4[start : start + dims.half, :]
            else:
                start = tap_phase(tap)[0] * dims.half
                left = a4[start : start + dims.half, :]
            product = dot_tn(left, right).astype(BF16)
            if tap < TAPS_Q:
                store_cuts(outs[stem + "q"], tap * shard, product, dims.cuts)
            else:
                at = blocks6 * shard6 + (tap - TAPS_Q) * shard
                store_cuts(outs[stem + "p"], at, product, dims.cuts)
        if stem == "keep":
            outs.start()


def four_back_body(dims, place_ref, ins, outs, shifted, four_grad):
    ins.start()
    dz4, norm_grad = outs.dz4, outs.norm4
    hot, dz5, z4, phase_mask = ins.hot, ins.dz5, ins.z4, ins.phase_mask
    full_count, _ = counts(place_ref, dims.crops)
    width = dims.widths[3]
    for place in range(3):
        rows = slice(place * dims.half, (place + 1) * dims.half)
        shifted[rows, :] = dot(hot[FORE_SHIFT + place], dz5[...]).astype(BF16)
    _, _, slope, offset = affine(dims, 3, ins.stats, ins.n4)
    sums = Sums(width)
    for phase, tile in enumerate(pieces(0, dims.full, dims.half)):
        for block in pieces(0, width, BLOCK):
            grad = 0.0
            for tap in range(9):
                own, (row_shift, col_shift_) = tap_phase(tap)
                if own != phase:
                    continue
                if tap in SHIFTED:
                    start = (2 * row_shift + col_shift_ - 1) * dims.half
                    left = shifted[start : start + dims.half, :]
                else:
                    left = dz5[...]
                grad += dot_nt(left, ins.part("w5", tap)[block, :])
            zone = z4[tile, block]
            grad = grad * wide(phase_mask[tile, :], BLOCK)
            grad = grad * silu_slope(zone * slope[:, block] + offset[:, block])
            four_grad[tile, block] = grad
            sums.add(block, grad, grad * zone)
    line = norm_back_lines(sums.get(), ins.n4, ins.stats, dims, 3, full_count, norm_grad)
    for rows in pieces(0, dims.full, ROWS):
        values = four_grad[rows, :] * line[0] + line[1] - z4[rows, :] * line[2]
        dz4[rows, :] = (wide(phase_mask[rows, :], width) * values).astype(BF16)


def middle_back_body(dims, place_ref, ins, outs, phase_grad):
    ins.start()
    both, joined_grad, dz3, norm_grad = (outs[name] for name in ("both34", "joined", "dz3", "norm3"))
    dz4, v4, strided, mid, a2 = (ins[name] for name in ("dz4", "v4", "strided", "mid", "a2"))
    hot, z3, xm, full_mask = ins.hot, ins.z3, ins.xm, ins.full_mask
    crops, pixels, half_pixels = dims.crops, dims.pixels, dims.half_pixels
    full_count, _ = counts(place_ref, crops)
    width = dims.widths[2]

    columns = both.shape[3]
    shard = dims.widths[2] // dims.cuts
    for rows in pieces(0, width, 2 * shard):
        for half, product in enumerate(halves(dot_tn(mid[:, rows], dz4[...]))):
            for cut, part in enumerate(pieces(0, 2 * shard, shard)):
                for place, block in enumerate(pieces(0, product.shape[1], columns)):
                    here = slice(place * shard, (place + 1) * shard)
                    both[half, rows.start // shard + cut, here] = product[part, block]

    for phase, tile in enumerate(pieces(0, dims.full, dims.half)):
        for block in pieces(0, width, BLOCK):
            grad = dot_nt(dz4[tile, :], v4[block, :])
            if phase == 0:
                grad += strided[:, block]
            phase_grad[tile, block] = grad.astype(BF16)

    _, _, slope, offset = affine(dims, 2, ins.stats, ins.n3)
    sums = Sums(width)
    for crop, tile in enumerate(pieces(0, dims.full, pixels)):
        for block in pieces(0, width, BLOCK):
            starts = [phase * dims.half + crop * half_pixels for phase in range(4)]
            cells = [phase_grad[start : start + half_pixels, block] for start in starts]
            joined_grad[tile, block] = dot(hot[UNPHASED], jnp.concatenate(cells, axis=0))
        for rows in pieces(tile.start, pixels, 16):
            zone = z3[rows, :].astype(F32)
            value = xm[rows, :].astype(F32) + (zone * slope + offset)
            grad = joined_grad[rows, :] * silu_slope(value)
            joined_grad[rows, :] = grad
            sums.add(slice(0, width), grad, grad * zone)
    line = norm_back_lines(sums.get(), ins.n3, ins.stats, dims, 2, full_count, norm_grad)
    for rows in pieces(0, dims.full, 16):
        values = joined_grad[rows, :] * line[0] + line[1] - z3[rows, :].astype(F32) * line[2]
        dz3[rows, :] = (wide(full_mask[rows, :], width) * values).astype(BF16)

    half = width // 2
    shard3 = dims.widths[1] // dims.cuts
    start3 = shard * (dims.widths[3] // 2 // columns)
    turned = a2[...].T
    for which in range(2):
        for wide_block in range(half // BLOCK):
            start = which * half + wide_block * BLOCK
            product = dot(turned, dz3[:, start : start + BLOCK]).astype(BF16)
            for place, block in enumerate(pieces(0, BLOCK, columns)):
                at = start3 + (wide_block * (BLOCK // columns) + place) * shard3
                store_cuts(both.at[which], at, product[:, block], dims.cuts)


def last_body(dims, place_ref, ins, outs, one_grad, inputs_grad, framed, dz1, norm21, s1, both):
    strips = dims.strips
    norm_grad = norm21
    crops, pixels = dims.crops, dims.pixels
    full_count, _ = counts(place_ref, crops)
    me = place_ref[2 * crops]
    width = dims.widths[0]
    dz3, v3, z2, full_mask, hot, v2, z1, v1, joined_grad = (
        ins[name] for name in names(dz3=0, v3=0, z2=0, full_mask=0, hot=0, v2=0, z1=0, v1=0, joined=0).split()
    )
    tiles = pieces(0, dims.full, pixels)
    whole = slice(0, width)

    _, _, slope, offset = affine(dims, 1, ins.stats, ins.n2)
    sums = Sums(width)
    for tile in tiles:
        zone = z2[tile, :]
        grad = dot_nt(dz3[tile, :], v3[...])
        grad = grad * silu_slope(zone * slope + offset)
        one_grad[tile, :] = grad
        sums.add(whole, grad, grad * zone)
    line = norm_back_lines(sums.get(), ins.n2, ins.stats, dims, 1, full_count, norm_grad)
    blank_frame(dims, framed, 3 * width)
    for crop, tile in enumerate(tiles):
        start = crop * dims.padded + dims.map_cols
        for rows, target in zip(pieces(tile.start, pixels, ROWS), pieces(start, pixels, ROWS)):
            values = one_grad[rows, :] * line[0] + line[1] - z2[rows, :] * line[2]
            framed[target, whole.stop : 2 * width] = (wide(full_mask[rows, :], width) * values).astype(BF16)
        rows = slice(start, start + pixels)
        values = framed[rows, width : 2 * width]
        framed[rows, :width] = dot(hot[AFTER], values).astype(BF16)
        framed[rows, 2 * width :] = dot(hot[BEFORE], values).astype(BF16)

    _, _, slope, offset = affine(dims, 0, ins.stats, ins.n1)
    sums = Sums(width)
    for crop, tile in enumerate(tiles):
        grad = 0.0
        for tap in range(9):
            down, across = tap // 3, tap % 3
            start = crop * dims.padded + (2 - down) * dims.map_cols
            left = framed[start : start + pixels, across * width : (across + 1) * width]
            grad += dot_nt(left, v2[tap * width : (tap + 1) * width, :])
        zone = z1[tile, :]
        grad = grad * wide(full_mask[tile, :], width) * silu_slope(zone * slope + offset)
        one_grad[tile, :] = grad
        sums.add(whole, grad, grad * zone)
    line = norm_back_lines(sums.get(), ins.n1, ins.stats, dims, 0, full_count, norm_grad, width)
    for tile in tiles:
        for rows in pieces(tile.start, pixels, ROWS):
            values = one_grad[rows, :] * line[0] + line[1] - z1[rows, :] * line[2]
            dz1[rows, :] = (wide(full_mask[rows, :], width) * values).astype(BF16)
        for block in pieces(0, dims.widths[2], BLOCK):
            grad = dot_nt(dz1[tile, :], v1[block, :]) + joined_grad[tile, block]
            inputs_grad[tile, block] = grad.astype(BF16)
    for step in range(strips):
        strip = me ^ step
        for crop in range(crops):
            rows = pl.ds(pl.multiple_of(crop * pixels + strip * dims.strip, dims.strip), dims.strip)
            start = (step % 2 * crops + crop) * dims.strip if step > 1 else crop * dims.strip
            outs[STRIPS[step]][start : start + dims.strip, :] = inputs_grad[rows, :]
    first_weights(dims, place_ref, ins, outs, framed, dz1, norm21, s1, both)


def norm_rows(dims):
    rows = [
        (norm, kind, row)
        for norm, width in enumerate(dims.widths)
        for kind in range(2)
        for row in range(max(1, width // dims.cuts // LANES))
    ]
    middle = (len(rows) + 1) // 2
    return rows[:middle], rows[middle:]


NORM_ROWS = 16


def norm_source(dims, norm):
    places = [("norm21", 1), ("norm21", None), ("norm3", None), ("norm4", None), ("norm5", None)]
    name, behind = (places + [("norm67", None), ("norm67", 5)])[norm]
    return name, 0 if behind is None else dims.widths[behind]


def first_weights(dims, place_ref, ins, outs, framed, dz1, norm21, s1, both):
    a1, hot, xm = (ins[name] for name in names(a1=0, hot=0, xm=0).split())
    blank_frame(dims, s1, 3 * dims.widths[0])
    for crop, tile in enumerate(pieces(0, dims.full, dims.pixels)):
        start = crop * dims.padded + dims.map_cols
        for place, shift in enumerate((BEFORE, None, AFTER)):
            cells = a1[tile, :] if shift is None else dot(hot[shift], a1[tile, :]).astype(BF16)
            here = slice(place * dims.widths[0], (place + 1) * dims.widths[0])
            s1[start : start + dims.pixels, here] = cells
    start2 = ins.both34.shape[2]
    both[:, :, :start2] = ins.both34[...]
    width = dims.widths[0]
    shard2, shard1 = width // dims.cuts, dims.widths[2] // dims.cuts
    row = dims.map_cols
    span = dims.crops * dims.padded - 2 * row
    for down in range(3):
        left = s1[down * row : down * row + span, :]
        for half, product in enumerate(halves(dot_tn(left, framed[row : row + span, width : 2 * width]))):
            for across in range(3):
                at = start2 + (3 * down + across) * shard2
                store_cuts(both.at[half], at, product[across * width : (across + 1) * width], dims.cuts)
    start = start2 + 9 * shard2
    for rows in pieces(0, dims.cuts * shard1, 2 * shard1):
        for half, product in enumerate(halves(dot_tn(xm[:, rows], dz1[...]))):
            for cut, part in enumerate(pieces(0, 2 * shard1, shard1)):
                both[half, rows.start // shard1 + cut, start : start + shard1] = product[part]
    start += shard1
    for cut in range(dims.cuts):
        for half, rows in enumerate(norm_rows(dims)):
            lines = []
            for norm, kind, row in rows:
                name, at = norm_source(dims, norm)
                at += cut * dims.widths[norm] // dims.cuts // LANES * LANES + row * LANES
                source = norm21 if name == "norm21" else ins[name]
                lines.append(source[kind : kind + 1, at : at + LANES])
            lines.append(jnp.zeros((NORM_ROWS - len(lines), LANES), F32))
            both[half, cut, start:] = jnp.concatenate(lines, axis=0).astype(BF16)
    core = place_ref[2 * dims.crops] & 1
    for half in range(2):

        @pl.when(core == half)
        def _(half=half):
            outs.keep[...] = both[half]
            middle = dims.cuts // 2
            outs.send0[...] = both[1 - half, :middle]
            outs.send1[...] = both[1 - half, middle:]


def place_call(dims, kept):
    size = dims.pixels
    outs = dict(
        full_mask=((dims.full, LANES), F32),
        phase_mask=((dims.full, LANES), F32),
        half_mask=((dims.half, LANES), F32),
        hot=((HOTS, size, size), BF16),
    )
    return flow("place", place_body, dims, kept, {}, outs)


def named(stem, values):
    return {f"{stem}{index}": value for index, value in enumerate(values)}


def pick(kept, names):
    return {name: kept[name] for name in names.split()}


def first_call(dims, x_blocks, kept):
    full, half, widths = dims.full, dims.half, dims.widths
    inputs = {**named("x", x_blocks), **pick(kept, names(w1=0, n1=0, w2=0, n2=0, w3=0, n3=0, w4=0, n4=0, w5=0, n5=0, w6=0, w7=0))}
    outs = dict(
        xm=((full, widths[2]), BF16),
        z1=((full, widths[0]), F32),
        a1=((full, widths[0]), BF16),
        z2=((full, widths[1]), F32),
        a2=((full, widths[1]), BF16),
        z3=((full, widths[2]), BF16),
        mid=((full, widths[2]), BF16),
        stats=((2, sum(widths)), F32),
        z4=((full, widths[3]), F32),
        a4=((full, widths[3]), BF16),
        sh4=((len(SHIFTED) * half, widths[3]), BF16),
        z5=((half, widths[4]), F32),
        a5=((half, widths[4]), BF16),
    )
    scratch = [((full, widths[2]), F32), ((2, dims.pixels, widths[2]), BF16)]
    scratch.append(((dims.crops * dims.padded, 3 * widths[0]), BF16))
    return flow("first", first_body, dims, kept, inputs, outs, scratch, "w1", share=names(w6=0, w7=0))


def second_call(dims, g_blocks, kept):
    half, widths, cuts = dims.half, dims.widths, dims.cuts
    inputs = {**named("g", g_blocks), **pick(kept, names(n6=0, n7=0))}
    weight = ((cuts, widths[2] // cuts * (widths[6] // 2 // BLOCK), BLOCK), BF16)
    outs = dict(
        keep7=weight,
        send7=weight,
        dz6=((half, widths[5]), BF16),
        dz7=((half, widths[6]), BF16),
        norm67=((2, 2 * widths[5]), F32),
    )
    strips = {name: ((half // dims.strips, widths[5]), BF16) for name in STRIPS[:2]}
    strips[STRIPS[2]] = ((half // dims.strips * 2, widths[5]), BF16)
    zone = ((2, half, BLOCK), F32)
    scratch = [((half, widths[5]), BF16)] * 2 + [zone, zone, ((half, BLOCK), F32), ((widths[2], half), BF16)]
    return flow("second", second_body, dims, kept, inputs, {**outs, **strips}, scratch)


def five_back(dims, kept):
    half, widths, cuts = dims.half, dims.widths, dims.cuts
    shard, columns = widths[3] // cuts, widths[4] // 2
    rows_p = widths[4] // cuts * (widths[5] // 2 // columns) + (9 - TAPS_Q) * shard
    outs = dict(
        keepp=((cuts, rows_p, columns), BF16),
        sendp=((cuts, rows_p, columns), BF16),
        keepq=((cuts, TAPS_Q * shard, columns), BF16),
        sendq=((cuts, TAPS_Q * shard, columns), BF16),
        strided=((half, widths[2]), F32),
        dz5=((half, widths[4]), BF16),
        norm5=((2, widths[4]), F32),
    )
    return flow("five", five_back_body, dims, kept, pick(kept, names(n5=0, w6=0)), outs, (), "w6")


def four_back(dims, kept):
    half, full, widths = dims.half, dims.full, dims.widths
    outs = dict(
        dz4=((full, widths[3]), BF16),
        norm4=((2, widths[3]), F32),
    )
    scratch = [((3 * half, widths[4]), BF16), ((full, widths[3]), F32)]
    return flow("four", four_back_body, dims, kept, pick(kept, names(n4=0, w5=0, w4=0)), outs, scratch, names(w5=0, w4=0), "", "w4")


def rows_34(dims):
    columns = dims.widths[0] // 2
    four = dims.widths[2] // dims.cuts * (dims.widths[3] // 2 // columns)
    three = dims.widths[1] // dims.cuts * (dims.widths[2] // 2 // columns)
    return four, three


def middle_back(dims, kept):
    full, widths, cuts = dims.full, dims.widths, dims.cuts
    weight = ((2, cuts, sum(rows_34(dims)), widths[0] // 2), BF16)
    outs = dict(
        both34=weight,
        joined=((full, widths[2]), F32),
        dz3=((full, widths[2]), BF16),
        norm3=((2, widths[2]), F32),
    )
    scratch = [((full, widths[2]), BF16)]
    inputs = pick(kept, names(n3=0, w3=0, w2=0, w1=0))
    return flow("middle", middle_back_body, dims, kept, inputs, outs, scratch, share=names(w3=0, w2=0, w1=0))


def last_back(dims, kept):
    full, widths, cuts = dims.full, dims.widths, dims.cuts
    strips = {name: ((full // dims.strips, widths[2]), BF16) for name in STRIPS[:2]}
    strips[STRIPS[2]] = ((full // dims.strips * 2, widths[2]), BF16)
    rows = sum(rows_34(dims)) + 9 * (widths[0] // cuts) + widths[2] // cuts + NORM_ROWS
    columns = widths[0] // 2
    outs = dict(
        keep=((cuts, rows, columns), BF16),
        send0=((cuts // 2, rows, columns), BF16),
        send1=((cuts // 2, rows, columns), BF16),
        **strips,
    )
    framed = ((dims.crops * dims.padded, 3 * widths[0]), BF16)
    scratch = [
        ((full, widths[0]), F32),
        ((full, widths[2]), BF16),
        framed,
        ((full, widths[0]), BF16),
        ((2, 2 * widths[0]), F32),
        framed,
        ((2, cuts, rows, columns), BF16),
    ]
    return flow("last", last_body, dims, kept, pick(kept, names(n2=0, n1=0)), outs, scratch)


class Job:
    def __init__(self, arrays, outer, inner, bit):
        self.arrays, self.outer, self.inner, self.bit = arrays, outer, inner, bit
        count, self.rows, self.columns = arrays[0].shape
        assert count == 2 * outer * inner
        assert len(arrays) == 2 or (inner == 1 and outer % 2 == 0)
        self.shape = (outer * inner, self.rows, self.columns)

    def step(self):
        if self.rows % 16:
            return self.rows
        most = max(16, (1 << 13) // self.columns)
        return max(size for size in range(16, self.rows + 1, 16) if self.rows % size == 0 and size <= most)


def add_call(place, groups, here):
    def kernel(place_ref, *refs):
        count = sum(len(job.arrays) for group in groups for job in group)
        sources, targets = refs[:count], refs[count:]
        for number, group in enumerate(groups):
            start = 0
            for job in group:
                (first, *seconds), sources = sources[: len(job.arrays)], sources[len(job.arrays) :]
                rank, shift = job.bit
                own = (place_ref[rank] >> shift) & 1
                for target, bit in ((targets[2 * number], 1 - own), (targets[2 * number + 1], own)):
                    for index in range(job.outer * job.inner):
                        outer, inner = index // job.inner, index % job.inner
                        source = (2 * outer + bit) * job.inner + inner
                        piece = outer * len(seconds) // job.outer
                        offset = piece * 2 * job.outer * job.inner // len(seconds)
                        size = job.step()

                        def add(
                            at,
                            _,
                            source=source,
                            offset=offset,
                            target=target,
                            index=index,
                            first=first,
                            second=seconds[piece],
                            size=size,
                            start=start,
                        ):
                            here_ = pl.ds(pl.multiple_of(at * size, size), size)
                            there = pl.ds(pl.multiple_of(start + at * size, 16 if size % 16 == 0 else 1), size)
                            value = first[source, here_, :].astype(F32) + second[source - offset, here_, :].astype(F32)
                            target[index, there, :] = value.astype(BF16)
                            return 0

                        lax.fori_loop(0, job.rows // size, add, 0)
                start += job.rows

    arrays = [value for group in groups for job in group for value in job.arrays]
    shapes = [
        (group[0].outer * group[0].inner, sum(job.rows for job in group), group[0].columns) for group in groups
    ]
    results = pl.pallas_call(
        kernel,
        out_shape=[
            (pltpu.VMEM if here else jax.ShapeDtypeStruct)(shape, BF16) for shape in shapes for _ in range(2)
        ],
        in_specs=[pl.BlockSpec(memory_space=pltpu.SMEM)] + [pl.BlockSpec(memory_space=pltpu.VMEM)] * len(arrays),
        out_specs=[pl.BlockSpec(memory_space=pltpu.VMEM)] * (2 * len(shapes)),
        compiler_params=pltpu.CompilerParams(
            vmem_limit_bytes=(4 if here else 16) * sum(math.prod(shape) for shape in shapes) + 2 * MIB
        ),
        cost_estimate=pl.CostEstimate(flops=FLOPS, bytes_accessed=0, transcendentals=0),
    )(place, *(pltpu.with_memory_space_constraint(value, pltpu.VMEM) if here else value for value in arrays))
    return list(zip(results[::2], results[1::2]))


def finish_call(dims, place, images, image_at, own, other):
    shards = [width // images for width in dims.widths]
    columns = own.shape[1]
    count4, count3 = dims.widths[3] // 2 // columns, dims.widths[2] // 2 // columns
    outs = [
        (shards[2], dims.widths[3]),
        (shards[1], dims.widths[2]),
        (9 * shards[0], dims.widths[1]),
        (shards[2], dims.widths[0]),
        *((2, shard) for shard in shards),
    ]

    def kernel(place_ref, own_ref, other_ref, four, three, two, one, *norms):
        core = place_ref[image_at - 1] & 1
        image = place_ref[image_at]

        def put(halves):
            at = 0
            for target, shard, count in ((four, shards[2], count4), (three, shards[1], count3)):
                for half, values in enumerate(halves):
                    for block in range(count):
                        start = (half * count + block) * columns
                        rows = slice(at + block * shard, at + (block + 1) * shard)
                        target[:, start : start + columns] = values[rows, :].astype(F32)
                at += count * shard
            for target in (two, one):
                size = target.shape[0]
                for half, values in enumerate(halves):
                    here = slice(half * columns, (half + 1) * columns)
                    target[:, here] = values[at : at + size, :].astype(F32)
                at += size
            cut = image * dims.cuts // images
            for values, rows in zip(halves, norm_rows(dims)):
                lines = values[at : at + NORM_ROWS, :].astype(F32)
                for index, (norm, kind, row) in enumerate(rows):
                    shard = shards[norm]
                    if shard >= LANES:
                        norms[norm][kind : kind + 1, row * LANES : (row + 1) * LANES] = lines[index : index + 1]
                        continue
                    lane = image * shard - cut * (dims.widths[norm] // dims.cuts) // LANES * LANES - row * LANES

                    @pl.when((lane >= 0) & (lane < LANES))
                    def _(lane=lane, norm=norm, kind=kind, index=index, shard=shard):
                        line = pltpu.roll(lines[index // 8 * 8 : index // 8 * 8 + 8], LANES - lane, 1)
                        norms[norm][kind : kind + 1, :] = line[index % 8 : index % 8 + 1, :shard]

        @pl.when(core == 0)
        def _():
            put((own_ref, other_ref))

        @pl.when(core == 1)
        def _():
            put((other_ref, own_ref))

    return pl.pallas_call(
        kernel,
        out_shape=[jax.ShapeDtypeStruct(shape, F32) for shape in outs],
        in_specs=[pl.BlockSpec(memory_space=pltpu.SMEM)] + [pl.BlockSpec(memory_space=pltpu.VMEM)] * 2,
        out_specs=[pl.BlockSpec(memory_space=pltpu.VMEM)] * len(outs),
        compiler_params=pltpu.CompilerParams(vmem_limit_bytes=8 * MIB),
        cost_estimate=pl.CostEstimate(flops=FLOPS, bytes_accessed=0, transcendentals=0),
    )(place, own, other)


def stack_call(dims, place, blocks, whole=None):
    me_at = 2 * dims.crops
    steps = list(blocks)
    count = len(steps)
    shape = (count, *blocks[steps[0]].shape)

    def kernel(place_ref, *refs):
        sources = refs[:count]
        target, held, in_sems, out_sems = refs[-4:]
        me = place_ref[me_at]
        loads = [
            pltpu.make_async_copy(source, held.at[index], in_sems.at[index])
            for index, source in enumerate(sources)
        ]
        stores = [
            pltpu.make_async_copy(held.at[index], target.at[me ^ step], out_sems.at[index])
            for index, step in enumerate(steps)
        ]
        for load in loads:
            load.start()
        for load, store in zip(loads, stores):
            load.wait()
            store.start()
        for store in stores:
            store.wait()

    given = [] if whole is None else [whole]
    return pl.pallas_call(
        kernel,
        out_shape=pltpu.HBM((dims.strips, *shape[1:]), BF16),
        in_specs=[pl.BlockSpec(memory_space=pltpu.SMEM)]
        + [pl.BlockSpec(memory_space=pl.ANY)] * count
        + [pl.BlockSpec(memory_space=pltpu.HBM)] * len(given),
        out_specs=pl.BlockSpec(memory_space=pltpu.HBM),
        input_output_aliases={count + 1: 0} if given else {},
        scratch_shapes=[pltpu.VMEM(shape, BF16)] + [pltpu.SemaphoreType.DMA((count,))] * 2,
        compiler_params=pltpu.CompilerParams(vmem_limit_bytes=2 * math.prod(shape) + MIB),
        cost_estimate=pl.CostEstimate(flops=FLOPS, bytes_accessed=0, transcendentals=0),
    )(place, *blocks.values(), *given)


def partner(count, step):
    return [(i, i ^ step) for i in range(count)]


def swap(value, axis, step):
    return lax.ppermute(value, axis, partner(lax.axis_size(axis), step))


def after(value, *tokens):
    return lax.optimization_barrier((value, *tokens))[0]


def exchange(parts, order):
    moved = dict.fromkeys(range(len(parts)))
    moved[0] = parts[0]
    for step in order:
        moved[step] = swap(parts[step], "rows", step)
    return [moved[step] for step in range(len(parts))]


class Results:
    def __init__(self, turns, dims, place, strips):
        self.turns, self.dims, self.place = turns, dims, place
        self.own, self.core, chip = (strips[name] for name in STRIPS[:3])
        self.chip = swap(chip, "rows", 2)
        self.steps = [self.hand_on, self.stack]

    def advance(self):
        self.steps.pop(0)()

    def hand_on(self):
        chip, core = self.turns.take((self.chip, self.core))
        rows = self.own.shape[0]
        self.near, far = chip[:rows], chip[rows:]
        self.turns.done(far)
        self.parts = {0: self.own, 1: swap(core, "rows", 1), 2: self.near, 3: swap(far, "rows", 1)}

    def stack(self):
        self.whole = stack_call(self.dims, self.place, self.turns.take(self.parts))
        self.turns.done(self.whole)


def strips_of(strips, rank, steps):
    parts = []
    for step in steps:
        part = lax.dynamic_index_in_dim(strips, rank ^ step, 0, keepdims=False)
        parts.append(part.reshape(-1, part.shape[-1]))
    return parts


TAIL = words("7 p p 7", "c x c p", "7 p c 7", "x p b c", "c")


class Turns:
    def __init__(self):
        self.token = None

    def take(self, values):
        if self.token is None:
            return values
        return lax.optimization_barrier((values, self.token))[0]

    def done(self, token):
        self.token = token


class Reduction:
    def __init__(self, turns, place, rank_at, steps, keep, *sends):
        self.turns, self.place, self.rank_at = turns, place, rank_at
        self.left = sorted((step for axis, step in steps if axis == "images"), reverse=True)
        self.over_rows = any(axis == "rows" for axis, _ in steps)
        self.steps = [*steps, "rows", "core"]
        self.joining = []
        self.terms = (keep, *sends)

    def next_job(self):
        axis, distance = self.steps[0]
        arrays, inner = self.terms, 1
        if axis == "rows":
            count, rows, columns = arrays[0].shape
            arrays = [value.reshape(2 * count, rows // 2, columns) for value in arrays]
        else:
            inner = 1 << len([step for step in self.left if step < distance])
        outer = arrays[0].shape[0] // (2 * inner)
        return Job(arrays, outer, inner, (self.rank_at[axis], log2(distance)))

    def pass_on(self, send, kept):
        axis, distance = self.steps.pop(0)
        if axis == "images":
            self.left.remove(distance)
        self.terms = (kept, swap(send, axis, distance))

    def advance(self):
        if self.steps[0] == "rows":
            self.steps.pop(0)
            first, second = self.turns.take(self.terms)
            total = (first.astype(F32) + second.astype(F32)).astype(BF16)[0]
            self.turns.done(total)
            self.terms = (total, swap(total, "rows", 2))
        elif self.steps[0] == "core":
            self.steps.pop(0)
            total, other = self.turns.take(self.terms)
            if self.over_rows:
                bit = lax.axis_index("rows") >> 1
                total = jnp.concatenate(
                    [jnp.where(bit == 0, total, other), jnp.where(bit == 0, other, total)], axis=0
                )
            else:
                total = (total.astype(F32) + other.astype(F32)).astype(BF16)
            self.turns.done(total)
            self.terms = (total, swap(total, "rows", 1))
        else:
            others, self.joining = self.joining, []
            assert all(sorted(one.steps[:-2]) == sorted(self.steps[:-2]) for one in others)
            jobs = [one.next_job() for one in (self, *others)]
            given = self.turns.take([job.arrays for job in jobs])
            rank, shift = jobs[0].bit
            own = (self.place[rank] >> shift) & 1
            halves = []
            for bit in (1 - own, own):
                parts = []
                for job, arrays in zip(jobs, given):
                    sum_ = 0.0
                    for value in arrays:
                        value = value.reshape(job.outer, 2, job.inner, job.rows, job.columns)
                        sum_ += lax.dynamic_index_in_dim(value, bit, 1, keepdims=False).astype(F32)
                    parts.append(sum_.astype(BF16).reshape(job.shape))
                halves.append(parts[0] if len(parts) == 1 else jnp.concatenate(parts, axis=1))
            self.turns.done(halves[0])
            self.pass_on(*halves)

    def finish(self):
        assert not self.steps
        total, other = self.turns.take(self.terms)
        core = lax.axis_index("rows") & 1
        low = jnp.where(core == 0, total, other).astype(F32)
        high = jnp.where(core == 0, other, total).astype(F32)
        return low, high


def together(turns, place, *groups, here=True):
    jobs = [[one.next_job() for one in group] for group in groups]
    given = turns.take([[job.arrays for job in group] for group in jobs])
    for group, own in zip(jobs, given):
        for job, arrays in zip(group, own):
            job.arrays = arrays
    totals = add_call(place, jobs, here)
    turns.done(totals[-1][0])
    for group, (send, kept) in zip(groups, totals):
        assert all(one.left == group[0].left and one.steps == group[0].steps for one in group)
        group[0].pass_on(send, kept)


def by_image(value, cuts, images, shards, copied=0):
    if cuts == images:
        return value
    blocks, start = [], 0
    for shard in shards:
        block = value[:, start : start + shard].reshape(images, -1, value.shape[2])
        blocks.append(block)
        start += shard
    if copied:
        blocks.append(jnp.repeat(value[:, start:], images // cuts, axis=0))
    return jnp.concatenate(blocks, axis=1)


def local(features, crop_rows, crop_cols, *rest):
    out_grad = rest[-1]
    weights, norms = list(rest[0:-1:2]), rest[1:-1:2]
    rank = lax.axis_index("rows")
    strips, images = lax.axis_size("rows"), lax.axis_size("images")
    assert features.shape[0] == strips == 4
    _, crops, strip_rows, map_cols, _ = features.shape
    widths = [norm.shape[0] for norm in norms]
    cuts = min(images, min(widths) // 32)
    dims = Dims(crops, strip_rows * strips, map_cols, strips, cuts, widths)

    place = jnp.concatenate(
        [
            lax.dynamic_index_in_dim(crop_rows, rank, 0, keepdims=False),
            lax.dynamic_index_in_dim(crop_cols, rank, 0, keepdims=False),
            rank.astype(jnp.int32)[None],
            lax.axis_index("images").astype(jnp.int32)[None],
        ]
    )
    parts = strips_of(features, rank, range(strips))
    far_blocks = [swap(parts[step], "rows", step) for step in (2, 3)]
    x_blocks = [parts[0], swap(parts[1], "rows", 1), *far_blocks]
    kept = {"place": place}
    for index, (weight, norm) in enumerate(zip(weights, norms)):
        if weight.ndim == 3:
            weight = weight.transpose(1, 0, 2).reshape(-1, weight.shape[2])
        kept[f"w{index + 1}"] = weight
        kept[f"n{index + 1}"] = norm.T
    place_call(dims, kept)
    early = (*x_blocks, kept["hot"], kept["w2"], kept["w5"])
    g_parts = strips_of(out_grad, rank, range(strips))
    g_blocks = exchange(after(g_parts, *early), (2, 3, 1))

    distances = [1 << bit for bit in range((images - 1).bit_length())]
    near = [("images", step) for step in distances]
    across = [("rows", 2)]
    turns = Turns()

    rank_at = {"rows": 2 * crops, "images": 2 * crops + 1}

    def reduction(steps, shards, keep, send):
        keep, send = (by_image(value, cuts, images, shards) for value in (keep, send))
        return Reduction(turns, place, rank_at, steps, keep, swap(send, "rows", 1))

    shard = [width // images for width in widths]
    cut = [width // cuts for width in widths]
    first_call(dims, x_blocks, kept)
    wide = second_call(dims, g_blocks, kept)
    block_out = Results(turns, dims, place, wide)
    sum7 = reduction(near, [cut[2]] * (widths[6] // 2 // BLOCK), wide["keep7"], wide["send7"])
    turns.done(wide["norm67"])
    kept["dz6"] = turns.take(kept["dz6"])
    five = five_back(dims, kept)
    shards_p = [cut[4]] * (widths[5] // widths[4]) + [cut[3]] * (9 - TAPS_Q)
    sum_p = reduction(across + near, shards_p, five["keepp"], five["sendp"])
    sum_q = reduction(near[1:2] + near[:1] + near[2:], [cut[3]] * TAPS_Q, five["keepq"], five["sendq"])
    turns.done(five["norm5"])
    together(turns, place, [sum7])
    kept["dz5"] = turns.take(kept["dz5"])
    turns.done(four_back(dims, kept)["norm4"])
    together(turns, place, [sum_p], [sum_q])
    block_out.advance()
    kept["dz4"] = turns.take(kept["dz4"])
    middle = middle_back(dims, kept)
    turns.done(middle["norm3"])
    kept["dz3"] = turns.take(kept["dz3"])
    last = last_back(dims, kept)
    inputs_grad = Results(turns, dims, place, last)
    columns = widths[0] // 2
    shards_c = [cut[2]] * (widths[3] // 2 // columns) + [cut[1]] * (widths[2] // 2 // columns)
    shards_c += [cut[0]] * 9 + [cut[2]]
    keep = by_image(last["keep"], cuts, images, shards_c, NORM_ROWS)
    sends = [by_image(last[name], cuts // 2, images // 2, shards_c, NORM_ROWS) for name in ("send0", "send1")]
    sum_c = Reduction(turns, place, rank_at, near, keep, *(swap(send, "rows", 1) for send in sends))
    turns.done(last["keep"])
    for group in ([sum7], [sum_q], [sum_p], [sum_c]):
        together(turns, place, group, here=False)
    sum7.joining = [sum_q]

    def joined(halves, start=0, size=None):
        return jnp.concatenate([half[start : start + size] if size else half[start:] for half in halves], axis=1)

    def blocks(halves, start, shard, count):
        return jnp.concatenate(
            [half[start + block * shard : start + (block + 1) * shard] for half in halves for block in range(count)],
            axis=1,
        )

    count6 = widths[5] // widths[4]
    done = {}

    def finish(name):
        if name == "7":
            halves, count = sum7.finish(), widths[6] // 2 // BLOCK
            done["7"], done["5q"] = blocks(halves, 0, shard[2], count), joined(halves, shard[2] * count)
        elif name == "p":
            halves = sum_p.finish()
            done["6"], done["5p"] = blocks(halves, 0, shard[4], count6), joined(halves, shard[4] * count6)
        elif name == "c":
            own, other = turns.take(sum_c.terms)
            done["c"] = finish_call(dims, place, images, rank_at["images"], own, other)
        if "5" not in done and "5q" in done and "5p" in done:
            done["5"] = jnp.concatenate([done["5q"], done["5p"]], axis=0)
        turns.done([value for value in done.values()])

    sums = {"7": sum7, "p": sum_p, "c": sum_c, "x": inputs_grad, "b": block_out}
    names = TAIL.split()
    while len(done) < 6 or any(total.steps for total in sums.values()):
        for name in names:
            if sums[name].steps:
                sums[name].advance()
            elif {"p": "6"}.get(name, name) not in done and name in "7pc":
                finish(name)
        names = sums
    dw5 = done["5"].reshape(9, shard[3], widths[4]).transpose(1, 0, 2)
    dw4, dw3, dw2, dw1, *norm_grads = done["c"]
    dw2 = dw2.reshape(9, shard[0], widths[1]).transpose(1, 0, 2)
    norm_grads = [value.T for value in norm_grads]
    grads = [dw1, dw2, dw3, dw4, done["6"], done["7"]]
    grads.insert(4, dw5)
    results = [value for pair in zip(grads, norm_grads) for value in pair]
    block_out = block_out.whole.reshape(out_grad.shape)
    features_grad = inputs_grad.whole.reshape(features.shape)
    return (block_out, features_grad, *results)


def solution(mesh):
    strips = P(None, "images", "rows", None, None)
    grads = [P("images", None)] * 14
    grads[2] = grads[8] = P("images", None, None)
    return jax.shard_map(
        local,
        mesh=mesh,
        in_specs=(strips, P(None, "images"), P(None, "images")) + (P(),) * 14 + (strips,),
        out_specs=(strips, strips, *grads),
        check_vma=False,
    )
```
